32 devices in a mesh: groups: 2 (over x), enc: 16 (over z, y, core).
Axes of the slice: x: 2, y: 2, z: 4, core: 2. Of those that a mesh axis runs over, the one named last changes fastest.
Arguments:
- cache_rows: bfloat16 [4096, 2, 1280], P(('groups', 'enc')), parts along dimension 0, may hold values from -6 to 6
- hit_owner: int32 [8192, 1], P(('groups', 'enc')), parts along dimension 0, may hold values from 0 to 15; in each aligned block of 256 rows (0 to 255, 256 to 511, ...) at most 32 rows name the same one
- hit_slot: int32 [8192], P(('groups', 'enc')), parts along dimension 0, may hold values from 0 to 127
- miss_pixels: bfloat16 [4096, 2, 588], P(('groups', 'enc')), parts along dimension 0, may hold values from -6 to 6
- miss_encoder: int32 [4096, 1], P(('groups', 'enc')), parts along dimension 0, may hold values from 0 to 15; in each aligned block of 128 rows (0 to 127, 128 to 255, ...) at most 16 rows name the same one
- patch_weight: bfloat16 [588, 1280], replicated, may hold values from -0.25 to 0.25
- position: float32 [2, 1280], replicated, may hold values from -6 to 6
- norm_gain: float32 [1280], replicated, may hold values from 0.1 to 1.9
- norm_bias: float32 [1280], replicated, may hold values from -3 to 3
- pair_weight: bfloat16 [1280, 2048], replicated, may hold values from -0.15625 to 0.15625
Outputs:
- hit_pairs: bfloat16 [8192, 2, 2048], P(('groups', 'enc')), parts along dimension 0
- miss_pairs: bfloat16 [4096, 2, 2048], P(('groups', 'enc')), parts along dimension 0
- fresh_cache: bfloat16 [8192, 2, 1280], P(('groups', 'enc')), parts along dimension 0
The draws below stay inside these ranges and needn't reach their ends.
There are 2 independent parts, one for each index of `groups`. The reference program is written for one: setup_inputs(seed, part) draws one part's arguments, and reference() takes and returns one part's arrays. A program takes and returns all parts, laid end to end along the dimension named above; an argument that names none is the same for every part. Nothing has to cross between parts.
Inputs may be any that keep to these rules, and one draw needn't show every extreme that they name: `hit_owner`: in the rows of one device no cache shard is named more than 32 times, and some device names one exactly 32 times. `miss_encoder`: in the rows of one device no encoder shard is named more than 16 times, and some device names one exactly 16 times.
All inputs are finite; a program needn't handle non-finite values.
Results may differ from the reference program's by a relative error of at most 0.0051.
Values may be sent and summed in bfloat16 or wider, within the bound.
A program may use at most 64 MiB of HBM per device.

```python
import math
import jax
import jax.numpy as jnp
import numpy as np
from jax import lax

E = 1280
KVW = 1024
PIX = 588
PATCH = 2
SLOTS = 128
HIT_DEV = 256
MISS_DEV = 128
CAP = 32
CAPM = 16
HITS = 4096
MISSES = 2048
CACHED = 2048
N_ENC = 16


def with_ends(values, own_key, low, high):
    place = [jax.random.randint(jax.random.fold_in(own_key, axis), (), 0, length) for axis, length in enumerate(values.shape)]
    main_axis = values.shape.index(max(values.shape))
    beside = place[:main_axis] + [(place[main_axis] + 1) % values.shape[main_axis]] + place[main_axis + 1:]
    return values.at[tuple(place)].set(low).at[tuple(beside)].set(high)


def block_scale(own_key, dims, pieces, least, largest):
    def one(dim, parts):
        draws = jax.random.uniform(jax.random.fold_in(jax.random.fold_in(own_key, 6), dim), (parts,), jnp.float32, least / len(pieces), largest / len(pieces))
        return jnp.repeat(jnp.exp(draws), dims[dim] // parts).reshape((-1,) + (1,) * (len(dims) - dim - 1))

    factor_of = one(*pieces[0])
    for cut in pieces[1:]:
        factor_of = factor_of * one(*cut)
    return factor_of


def assign_block(own_key, own, number, rows, count, top, most, skew):
    order = jax.random.permutation(own_key, count)
    heavy_load, common = portions_of(count, rows * top, most, skew, True), portions_of(count, rows * top, most, skew, False)
    places = jnp.arange(count)

    def named(sizes, offset_by):
        used = int((sizes > 0).sum())
        fixed = max(1, used // 4)
        shifted = fixed + (places - fixed + offset_by * (used - fixed)) % max(1, count - fixed)
        return jnp.zeros((count,), jnp.int32).at[order[jnp.where(places < fixed, places, shifted)]].set(jnp.asarray(sizes, jnp.int32))

    sizes = jnp.where(number % 4 == 0, named(heavy_load, number // 4), named(common, number - number // 4 - 1))
    mixed = jax.random.permutation(jax.random.fold_in(own, 3), count)
    giver, receiver = mixed[0:count // 2 * 2:2], mixed[1:count // 2 * 2:2]
    margin = jnp.minimum(sizes[giver] - 1, most - sizes[receiver]) // 2
    margin = jnp.where((giver == order[0]) | (receiver == order[0]) | (sizes[receiver] == 0), 0, jnp.maximum(margin, 0))
    shifted = jax.random.randint(jax.random.fold_in(own, 4), (count // 2,), 0, 1 << 20) % (margin + 1)
    sizes = sizes.at[giver].add(-shifted).at[receiver].add(shifted)
    labels = jnp.searchsorted(jnp.cumsum(sizes), jnp.arange(rows * top), side="right").astype(jnp.int32)
    table = labels.reshape(top, rows).T
    table = table[jax.random.permutation(jax.random.fold_in(own, 1), rows)]
    offset_by = jax.random.randint(jax.random.fold_in(own, 2), (rows, 1), 0, top)
    return jnp.take_along_axis(table, (jnp.arange(top)[None, :] + offset_by) % top, axis=1)


def portions_of(amount, total, most, lean, full):
    loads = [(1 << 20) // math.isqrt(grade ** lean) + 1 for grade in range(1, amount + 1)]
    largest = most if full else min(most, max(-(-total // amount), total * loads[0] // sum(loads)))
    least = 1 if total - largest >= amount - 1 else 0
    holding, surplus = [largest] + [least] * (amount - 1), total - largest - least * (amount - 1)
    while surplus > 0:
        candidates = [i for i in range(1, amount) if holding[i] < largest] or [i for i in range(1, amount) if holding[i] < most]
        pool, budget = sum([loads[i] for i in candidates]), surplus
        for i in candidates:
            more = min(most - holding[i], max(1, budget * loads[i] // pool), surplus)
            holding[i] = holding[i] + more
            surplus = surplus - more
    return np.array(holding)


def normal_values(key, dims, width, bound, split=(), held_as=jnp.bfloat16):
    drawn = width * jax.random.normal(key, dims, jnp.float32)
    if split:
        drawn = drawn * block_scale(key, dims, split, -0.22, 0.18)
    return jnp.clip(drawn, -bound, bound).astype(held_as)


def setup_inputs(seed: int = 0, part: int = 0) -> dict:
    splits = jax.random.split(jax.random.key(seed), 11)
    own_keys = jax.random.split(jax.random.fold_in(splits[10], part), 11)
    cache_rows = normal_values(own_keys[0], (CACHED, PATCH, E), 1.0, 6.0, ((0, 16),))
    hit_owner_keys = jax.random.split(jax.random.fold_in(own_keys[1], 1), HITS // HIT_DEV)
    hit_owner_turns = jax.random.permutation(jax.random.fold_in(own_keys[1], 3), HITS // HIT_DEV)
    hit_owner = jax.vmap(lambda own, number: assign_block(jax.random.fold_in(own_keys[1], 2), own, number, HIT_DEV, N_ENC, 1, CAP, 2))(hit_owner_keys, hit_owner_turns).reshape((HITS, 1))
    hit_slot = with_ends(jax.random.randint(own_keys[2], (HITS,), 0, SLOTS), jax.random.fold_in(own_keys[2], 1), 0, SLOTS - 1).astype(jnp.int32)
    miss_pixels = normal_values(own_keys[3], (MISSES, PATCH, PIX), 1.0, 6.0, ((0, 16),))
    miss_encoder_keys = jax.random.split(jax.random.fold_in(own_keys[4], 1), MISSES // MISS_DEV)
    miss_encoder_turns = jax.random.permutation(jax.random.fold_in(own_keys[4], 3), MISSES // MISS_DEV)
    miss_encoder = jax.vmap(lambda own, number: assign_block(jax.random.fold_in(own_keys[4], 2), own, number, MISS_DEV, N_ENC, 1, CAPM, 2))(miss_encoder_keys, miss_encoder_turns).reshape((MISSES, 1))
    patch_weight = normal_values(splits[5], (PIX, E), PIX ** -0.5, 0.25)
    position = normal_values(splits[6], (PATCH, E), 1.0, 6.0, (), jnp.float32)
    norm_gain = jnp.clip(1.0 + 0.18 * jax.random.normal(splits[7], (E,), jnp.float32), 0.1, 1.9)
    norm_bias = normal_values(splits[8], (E,), 0.5, 3.0, (), jnp.float32)
    pair_weight = normal_values(splits[9], (E, 2 * KVW), E ** -0.5, 0.15625)
    return dict(cache_rows=cache_rows, hit_owner=hit_owner, hit_slot=hit_slot, miss_pixels=miss_pixels, miss_encoder=miss_encoder, patch_weight=patch_weight, position=position, norm_gain=norm_gain, norm_bias=norm_bias, pair_weight=pair_weight)


def layer_norm(values, gain_row, bias_row):
    average = lax.optimization_barrier(jnp.mean(values, axis=-1, keepdims=True))
    centered = values - average
    variance = lax.optimization_barrier(jnp.mean(centered * centered, axis=-1, keepdims=True))
    return centered / jnp.sqrt(variance + 1e-05) * gain_row + bias_row

def encode_patches(pixel_rows, patch_weight, position, norm_gain, norm_bias):
    leading = pixel_rows.shape[:-1]
    flat_rows = pixel_rows.reshape(-1, pixel_rows.shape[-1])
    embedded = jnp.dot(flat_rows, patch_weight, preferred_element_type=jnp.float32)
    embedded = embedded.reshape(leading + (patch_weight.shape[1],)) + position
    return layer_norm(embedded, norm_gain, norm_bias).astype(jnp.bfloat16)

def project_pairs(embed_rows, pair_weight):
    leading = embed_rows.shape[:-1]
    flat_rows = embed_rows.reshape(-1, embed_rows.shape[-1])
    projected = jnp.dot(flat_rows, pair_weight, preferred_element_type=jnp.float32)
    return projected.astype(jnp.bfloat16).reshape(leading + (pair_weight.shape[1],))

def rank_within(targets):
    item_count = targets.shape[0]
    matches = targets[:, None] == targets[None, :]
    item_ids = jnp.arange(item_count, dtype=jnp.int32)
    earlier = item_ids[None, :] < item_ids[:, None]
    return lax.optimization_barrier(jnp.sum(jnp.where(matches & earlier, 1, 0), axis=1)).astype(jnp.int32)

def reference(cache_rows, hit_owner, hit_slot, miss_pixels, miss_encoder, patch_weight, position, norm_gain, norm_bias, pair_weight):
    hit_index = (hit_owner[:, 0] * SLOTS + hit_slot).astype(jnp.int32)
    hit_pairs = project_pairs(jnp.take(cache_rows, hit_index, axis=0), pair_weight)
    encoded = encode_patches(miss_pixels, patch_weight, position, norm_gain, norm_bias)
    miss_pairs = project_pairs(encoded, pair_weight)
    targets = miss_encoder[:, 0].reshape(N_ENC, MISS_DEV).astype(jnp.int32)
    ranking = jax.vmap(rank_within)(targets).reshape(-1)
    source_ids = jnp.arange(N_ENC * MISS_DEV, dtype=jnp.int32) // MISS_DEV
    destination = (targets.reshape(-1) * (N_ENC * CAPM) + source_ids * CAPM + ranking).astype(jnp.int32)
    fresh_cache = jnp.zeros((N_ENC * N_ENC * CAPM, PATCH, E), encoded.dtype).at[destination].set(encoded)
    return (hit_pairs, miss_pairs, fresh_cache)
```

```python
import jax
import jax.numpy as jnp
from jax import lax
from jax.sharding import PartitionSpec as P


def layer_norm(values, gain_row, bias_row):
    average = jnp.mean(values, axis=-1, keepdims=True)
    centered = values - average
    variance = jnp.mean(centered * centered, axis=-1, keepdims=True)
    return centered / jnp.sqrt(variance + 1e-05) * gain_row + bias_row


def encode_patches(pixel_rows, patch_weight, position, norm_gain, norm_bias):
    leading = pixel_rows.shape[:-1]
    flat_rows = pixel_rows.reshape(-1, pixel_rows.shape[-1])
    embedded = jnp.dot(flat_rows, patch_weight, preferred_element_type=jnp.float32)
    embedded = embedded.reshape(leading + (patch_weight.shape[1],)) + position
    return layer_norm(embedded, norm_gain, norm_bias).astype(jnp.bfloat16)


def project_pairs(embed_rows, pair_weight):
    leading = embed_rows.shape[:-1]
    flat_rows = embed_rows.reshape(-1, embed_rows.shape[-1])
    projected = jnp.dot(flat_rows, pair_weight, preferred_element_type=jnp.float32)
    return projected.astype(jnp.bfloat16).reshape(leading + (pair_weight.shape[1],))


def fill_places(targets, capacity):
    count = targets.shape[0]
    item = lax.broadcasted_iota(jnp.int32, (count, count), 1)
    row = lax.broadcasted_iota(jnp.int32, (count, count), 0)
    matches = targets[:, None] == targets[None, :]
    rank = jnp.sum(jnp.where(matches & (item < row), 1, 0), axis=1).astype(jnp.int32)
    return targets * capacity + rank


def slots_of(places, width):
    count = places.shape[0]
    return places[None, :] == lax.broadcasted_iota(jnp.int32, (width, count), 0)


def hits_by_gather(cache_rows, hit_owner, hit_slot, pair_weight):
    gathered = lax.all_gather(cache_rows, "enc", axis=0, tiled=True)
    rows = jnp.take(gathered, hit_owner * cache_rows.shape[0] + hit_slot, axis=0)
    return project_pairs(rows, pair_weight)


def hits_by_request(cache_rows, hit_owner, hit_slot, pair_weight):
    peers = lax.axis_size("enc")
    cap = max(2, 2 * hit_slot.shape[0] // peers)
    places = fill_places(hit_owner, cap)
    table = slots_of(places, peers * cap)
    wanted = jnp.sum(jnp.where(table, hit_slot[None, :], 0), axis=1).reshape(peers, cap)
    asked = lax.all_to_all(wanted, "enc", split_axis=0, concat_axis=0, tiled=True)
    stored = jnp.take(cache_rows, asked.reshape(-1), axis=0)
    stored = stored.reshape((peers, cap) + cache_rows.shape[1:])
    answered = lax.all_to_all(stored, "enc", split_axis=0, concat_axis=0, tiled=True)
    answered = answered.reshape((peers * cap,) + answered.shape[2:])
    return project_pairs(jnp.take(answered, places, axis=0), pair_weight)


def local(
    cache_rows,
    hit_owner,
    hit_slot,
    miss_pixels,
    miss_encoder,
    patch_weight,
    position,
    norm_gain,
    norm_bias,
    pair_weight,
):
    peers = lax.axis_size("enc")
    count, patches, pixels = miss_pixels.shape
    cap = max(2, 2 * count // peers)
    width = peers * cap
    table = slots_of(fill_places(miss_encoder[:, 0], cap), width).astype(jnp.bfloat16)
    items = jnp.concatenate(
        [miss_pixels.reshape(count, patches * pixels), jnp.ones((count, 1), jnp.bfloat16)], axis=1
    )
    outgoing = jnp.dot(table, items, preferred_element_type=jnp.float32).astype(jnp.bfloat16)
    outgoing = outgoing.reshape(peers, cap, items.shape[1])
    incoming = lax.all_to_all(outgoing, "enc", split_axis=0, concat_axis=0, tiled=True)
    incoming = incoming.reshape(width, items.shape[1])
    encode = lambda rows: encode_patches(rows, patch_weight, position, norm_gain, norm_bias)
    hits = hits_by_gather if peers <= 16 else hits_by_request
    hit_pairs = hits(cache_rows, hit_owner[:, 0], hit_slot, pair_weight)
    miss_pairs = project_pairs(encode(miss_pixels), pair_weight)
    fresh = encode(incoming[:, : patches * pixels].reshape(width, patches, pixels))
    live = incoming[:, patches * pixels :].reshape(width, 1, 1) > 0
    fresh_cache = jnp.where(live, fresh, jnp.zeros_like(fresh))
    return (hit_pairs, miss_pairs, fresh_cache)


def solution(mesh):
    placed = (
        P(("groups", "enc"), None, None),
        P(("groups", "enc"), None),
        P(("groups", "enc")),
        P(("groups", "enc"), None, None),
        P(("groups", "enc"), None),
        P(),
        P(),
        P(),
        P(),
        P(),
    )
    return jax.shard_map(
        local,
        mesh=mesh,
        in_specs=placed,
        out_specs=(
            P(("groups", "enc"), None, None),
            P(("groups", "enc"), None, None),
            P(("groups", "enc"), None, None),
        ),
        check_vma=False,
    )
```

```python
import functools

import jax
import jax.numpy as jnp
from jax import lax
from jax.experimental import pallas as pl
from jax.experimental.pallas import tpu as pltpu
from jax.sharding import PartitionSpec as P


def layer_norm(values, gain_row, bias_row):
    average = jnp.mean(values, axis=-1, keepdims=True)
    centered = values - average
    variance = jnp.mean(centered * centered, axis=-1, keepdims=True)
    return centered / jnp.sqrt(variance + 1e-05) * gain_row + bias_row


def encode_patches(pixel_rows, patch_weight, position, norm_gain, norm_bias):
    leading = pixel_rows.shape[:-1]
    flat_rows = pixel_rows.reshape(-1, pixel_rows.shape[-1])
    embedded = jnp.dot(flat_rows, patch_weight, preferred_element_type=jnp.float32)
    embedded = embedded.reshape(leading + (patch_weight.shape[1],)) + position
    return layer_norm(embedded, norm_gain, norm_bias).astype(jnp.bfloat16)


def project_pairs(embed_rows, pair_weight):
    leading = embed_rows.shape[:-1]
    flat_rows = embed_rows.reshape(-1, embed_rows.shape[-1])
    projected = jnp.dot(flat_rows, pair_weight, preferred_element_type=jnp.float32)
    return projected.astype(jnp.bfloat16).reshape(leading + (pair_weight.shape[1],))


def fill_places(targets, capacity):
    count = targets.shape[0]
    item = lax.broadcasted_iota(jnp.int32, (count, count), 1)
    row = lax.broadcasted_iota(jnp.int32, (count, count), 0)
    matches = targets[:, None] == targets[None, :]
    rank = jnp.sum(jnp.where(matches & (item < row), 1, 0), axis=1).astype(jnp.int32)
    return targets * capacity + rank


def slots_of(places, width):
    count = places.shape[0]
    return places[None, :] == lax.broadcasted_iota(jnp.int32, (width, count), 0)


def hits_by_request(cache_rows, hit_owner, hit_slot, pair_weight):
    peers = lax.axis_size("enc")
    cap = max(2, 2 * hit_slot.shape[0] // peers)
    places = fill_places(hit_owner, cap)
    table = slots_of(places, peers * cap)
    wanted = jnp.sum(jnp.where(table, hit_slot[None, :], 0), axis=1).reshape(peers, cap)
    asked = lax.all_to_all(wanted, "enc", split_axis=0, concat_axis=0, tiled=True)
    stored = jnp.take(cache_rows, asked.reshape(-1), axis=0)
    stored = stored.reshape((peers, cap) + cache_rows.shape[1:])
    answered = lax.all_to_all(stored, "enc", split_axis=0, concat_axis=0, tiled=True)
    answered = answered.reshape((peers * cap,) + answered.shape[2:])
    return project_pairs(jnp.take(answered, places, axis=0), pair_weight)


MESH = pl.DeviceIdType.MESH
HALVES = 2


def ring_place(chip, chips):
    z, y = chip // 2, chip % 2
    return y * (chips - 1) + z * (1 - 2 * y)


def ring_chip(place, chips):
    y = place // (chips // 2)
    z = y * (chips - 1) + place * (1 - 2 * y)
    return 2 * z + y


def ring_kernel(
    peers,
    pixels,
    cap,
    cache_ref,
    wanted_ref,
    places_ref,
    pixel_ref,
    patch_ref,
    position_ref,
    gain_ref,
    bias_ref,
    pair_hbm,
    hit_ref,
    miss_ref,
    fresh_ref,
    held,
    pair_ref,
    chosen,
    encoded,
    outgoing,
    incoming,
    up_send,
    up_recv,
    down_send,
    down_recv,
    side_send,
    side_recv,
    pixel_send,
    pixel_recv,
    load_sem,
    own_sem,
):
    chips = peers // 2
    slots, width = cache_ref.shape
    half = slots // HALVES
    embed = width // 2
    span = pixel_ref.shape[1] // 2
    pairs = pair_ref.shape[1]
    steps = chips - 1
    me = lax.axis_index("enc")
    chip, core = me // 2, me % 2
    place = ring_place(chip, chips)
    above = 2 * ring_chip((place + 1) % chips, chips) + core
    below = 2 * ring_chip((place + chips - 1) % chips, chips) + core
    beside = 2 * chip + 1 - core

    barrier = pltpu.get_barrier_semaphore()

    def greet(t, carry):
        pl.semaphore_signal(
            barrier, inc=1, device_id={"enc": (me + t) % peers}, device_id_type=MESH
        )
        return carry

    lax.fori_loop(1, peers, greet, 0)
    load = pltpu.make_async_copy(pair_hbm, pair_ref, load_sem)
    load.start()
    held[place, pl.ds(core * slots, slots), :] = cache_ref[...]
    rows = lax.broadcasted_iota(jnp.int32, (peers * cap, places_ref.shape[1]), 0)
    table = jnp.where(rows == places_ref[...], 1.0, 0.0).astype(jnp.bfloat16)
    outgoing[...] = jnp.dot(
        table, pixel_ref[...], preferred_element_type=jnp.float32
    ).astype(jnp.bfloat16)
    pl.semaphore_wait(barrier, peers - 1)

    def chunk(owner_place, owner_core, part):
        return held.at[owner_place, pl.ds(owner_core * slots + part * half, half), :]

    def move(ref, send_sem, recv_sem, target):
        return pltpu.make_async_remote_copy(
            src_ref=ref,
            dst_ref=ref,
            send_sem=send_sem,
            recv_sem=recv_sem,
            device_id={"enc": target},
            device_id_type=MESH,
        )

    def up(j, distance):
        return move(
            chunk((place + chips - distance) % chips, core, j % 2),
            up_send.at[j],
            up_recv.at[j],
            above,
        )

    def down(j, distance):
        return move(
            chunk((place + distance) % chips, core, 1 - j % 2),
            down_send.at[j],
            down_recv.at[j],
            below,
        )

    def side(k, whose):
        if k < 2:
            ref = chunk(place, whose, k)
        elif k % 2 == 0:
            j = (k - 2) // 2
            ref = chunk((place + chips - j // 2 - 1) % chips, whose, j % 2)
        else:
            j = (k - 3) // 2
            ref = chunk((place + j // 2 + 1) % chips, whose, 1 - j % 2)
        return move(ref, side_send.at[k], side_recv.at[k], beside)

    sent = []

    def start(copy):
        copy.start()
        sent.append(copy)

    for j in range(2):
        start(up(j, 0))
        start(down(j, 0))
    for j in range(2):
        start(side(j, core))

    def pixel_copy(t, target, source):
        return pltpu.make_async_remote_copy(
            src_ref=outgoing.at[pl.ds(target * cap, cap), :],
            dst_ref=incoming.at[pl.ds(source * cap, cap), :],
            send_sem=pixel_send.at[t],
            recv_sem=pixel_recv.at[t],
            device_id={"enc": target},
            device_id_type=MESH,
        )

    def send_pixels(t, carry):
        pixel_copy(t, (me + t) % peers, me).start()
        return carry

    lax.fori_loop(1, peers, send_pixels, 0)
    own = pltpu.make_async_copy(
        outgoing.at[pl.ds(me * cap, cap), :], incoming.at[pl.ds(me * cap, cap), :], own_sem
    )
    own.start()

    def encode(values, patch):
        embedded = jnp.dot(values, patch_ref[...], preferred_element_type=jnp.float32)
        embedded = embedded + position_ref[pl.ds(patch, 1), :]
        return layer_norm(embedded, gain_ref[...], bias_ref[...]).astype(jnp.bfloat16)

    def lanes(index, size):
        return pl.ds(pl.multiple_of(index * size, size), size)

    def encode_own(patch, carry):
        encoded[:, lanes(patch, embed)] = encode(pixel_ref[:, lanes(patch, span)], patch)
        return carry

    tile = 512
    tiles = pairs // tile

    def project(source, target):
        def one(i, carry):
            patch, column = i // tiles, i % tiles
            target[:, lanes(i, tile)] = jnp.dot(
                source[:, lanes(patch, embed)],
                pair_ref[:, lanes(column, tile)],
                preferred_element_type=jnp.float32,
            ).astype(jnp.bfloat16)
            return carry

        lax.fori_loop(0, 2 * tiles, one, 0)

    block = incoming.shape[0] // 2

    def encode_fresh(i, carry):
        patch, part = i // 2, i % 2
        here = pl.ds(pl.multiple_of(part * block, block), block)
        live = incoming[here, pixels : pixels + 1].astype(jnp.float32) > 0
        fresh = encode(incoming[here, lanes(patch, span)], patch)
        fresh_ref[here, lanes(patch, embed)] = jnp.where(live, fresh, jnp.zeros_like(fresh))
        return carry

    def choose(owner_place, first):
        column = lax.broadcasted_iota(jnp.int32, (wanted_ref.shape[0], 2 * slots), 1)
        column = column + owner_place * (2 * slots)
        pick = jnp.where(wanted_ref[...] == column, 1.0, 0.0).astype(jnp.bfloat16)

        def one(i, carry):
            found = jnp.dot(
                pick, held[owner_place, :, lanes(i, tile)], preferred_element_type=jnp.float32
            ).astype(jnp.bfloat16)
            if first:
                chosen[:, lanes(i, tile)] = found
            else:
                chosen[:, lanes(i, tile)] += found
            return carry

        lax.fori_loop(0, width // tile, one, 0)

    def wait_side(*copies):
        for k in copies:
            side(k, 1 - core).wait_recv()

    lax.fori_loop(0, 2, encode_own, 0)
    for j in range(steps):
        up(j, j // 2 + 1).wait_recv()
        if j + 2 < steps:
            start(up(j + 2, j // 2 + 1))
        start(side(2 + 2 * j, core))
        down(j, j // 2 + 1).wait_recv()
        if j + 2 < steps:
            start(down(j + 2, j // 2 + 1))
        start(side(3 + 2 * j, core))
        if j == 0:
            load.wait()
            project(encoded, miss_ref)
        elif j == 1:
            wait_side(0, 1)
            choose(place, True)
        elif j == steps - 2:

            def take_pixels(t, carry):
                pixel_copy(t, me, (me + peers - t) % peers).wait_recv()
                return carry

            lax.fori_loop(1, peers, take_pixels, 0)
            own.wait()
            lax.fori_loop(0, 4, encode_fresh, 0)
        elif j % 2 == 0:
            distance = j // 2
            wait_side(*range(4 * distance - 2, 4 * distance + 2))
            choose((place + chips - distance) % chips, False)
            choose((place + distance) % chips, False)
    wait_side(2 * steps, 2 * steps + 1)
    choose((place + chips // 2) % chips, False)
    project(chosen, hit_ref)
    for copy in sent:
        copy.wait_send()

    def end_pixels(t, carry):
        pixel_copy(t, (me + t) % peers, me).wait_send()
        return carry

    lax.fori_loop(1, peers, end_pixels, 0)


def by_ring(
    cache_rows,
    hit_owner,
    hit_slot,
    miss_pixels,
    miss_encoder,
    patch_weight,
    position,
    norm_gain,
    norm_bias,
    pair_weight,
):
    peers = lax.axis_size("enc")
    slots, patches, embed = cache_rows.shape
    hits = hit_slot.shape[0]
    count, _, pixels = miss_pixels.shape
    pairs = pair_weight.shape[1]
    cap = 2 * count // peers
    span = -(-(pixels + 1) // 128) * 128
    owner = hit_owner[:, 0]
    place = ring_place(owner // 2, peers // 2) * 2 + owner % 2
    wanted = (place * slots + hit_slot).reshape(hits, 1)
    places = fill_places(miss_encoder[:, 0], cap).reshape(1, count)
    spare = ((0, 0), (0, 0), (0, span - pixels))
    items = jnp.pad(miss_pixels, spare, constant_values=1).reshape(count, patches * span)
    patch_rows = jnp.pad(patch_weight, ((0, span - pixels), (0, 0)))
    bf16 = jnp.bfloat16
    vmem = pl.BlockSpec(memory_space=pltpu.VMEM)
    dma = pltpu.SemaphoreType.DMA
    steps = peers // 2 - 1
    hit_pairs, miss_pairs, fresh_cache = pl.pallas_call(
        functools.partial(ring_kernel, peers, pixels, cap),
        out_shape=(
            jax.ShapeDtypeStruct((hits, patches * pairs), bf16),
            jax.ShapeDtypeStruct((count, patches * pairs), bf16),
            jax.ShapeDtypeStruct((peers * cap, patches * embed), bf16),
        ),
        in_specs=[vmem] * 8 + [pl.BlockSpec(memory_space=pl.ANY)],
        out_specs=(vmem, vmem, vmem),
        scratch_shapes=[
            pltpu.VMEM((peers // 2, 2 * slots, patches * embed), bf16),
            pltpu.VMEM(pair_weight.shape, bf16),
            pltpu.VMEM((hits, patches * embed), bf16),
            pltpu.VMEM((count, patches * embed), bf16),
            pltpu.VMEM((peers * cap, patches * span), bf16),
            pltpu.VMEM((peers * cap, patches * span), bf16),
            dma((steps,)),
            dma((steps,)),
            dma((steps,)),
            dma((steps,)),
            dma((2 * steps + 2,)),
            dma((2 * steps + 2,)),
            dma((peers,)),
            dma((peers,)),
            dma,
            dma,
        ],
        compiler_params=pltpu.CompilerParams(
            collective_id=0, has_side_effects=True, vmem_limit_bytes=44 * 1024 * 1024
        ),
        cost_estimate=pl.CostEstimate(
            flops=2 * 2 * (hits + count) * embed * pairs,
            bytes_accessed=16 * 1024 * 1024,
            transcendentals=0,
        ),
    )(
        cache_rows.reshape(slots, patches * embed),
        wanted,
        places,
        items,
        patch_rows,
        position,
        norm_gain.reshape(1, embed),
        norm_bias.reshape(1, embed),
        pair_weight,
    )
    return (
        hit_pairs.reshape(hits, patches, pairs),
        miss_pairs.reshape(count, patches, pairs),
        fresh_cache.reshape(peers * cap, patches, embed),
    )


def local(
    cache_rows,
    hit_owner,
    hit_slot,
    miss_pixels,
    miss_encoder,
    patch_weight,
    position,
    norm_gain,
    norm_bias,
    pair_weight,
):
    peers = lax.axis_size("enc")
    count, patches, pixels = miss_pixels.shape
    cap = max(2, 2 * count // peers)
    width = peers * cap
    table = slots_of(fill_places(miss_encoder[:, 0], cap), width).astype(jnp.bfloat16)
    items = jnp.concatenate(
        [miss_pixels.reshape(count, patches * pixels), jnp.ones((count, 1), jnp.bfloat16)], axis=1
    )
    outgoing = jnp.dot(table, items, preferred_element_type=jnp.float32).astype(jnp.bfloat16)
    outgoing = outgoing.reshape(peers, cap, items.shape[1])
    incoming = lax.all_to_all(outgoing, "enc", split_axis=0, concat_axis=0, tiled=True)
    incoming = incoming.reshape(width, items.shape[1])
    encode = lambda rows: encode_patches(rows, patch_weight, position, norm_gain, norm_bias)
    hit_pairs = hits_by_request(cache_rows, hit_owner[:, 0], hit_slot, pair_weight)
    miss_pairs = project_pairs(encode(miss_pixels), pair_weight)
    fresh = encode(incoming[:, : patches * pixels].reshape(width, patches, pixels))
    live = incoming[:, patches * pixels :].reshape(width, 1, 1) > 0
    fresh_cache = jnp.where(live, fresh, jnp.zeros_like(fresh))
    return (hit_pairs, miss_pairs, fresh_cache)


def solution(mesh):
    placed = (
        P(("groups", "enc"), None, None),
        P(("groups", "enc"), None),
        P(("groups", "enc")),
        P(("groups", "enc"), None, None),
        P(("groups", "enc"), None),
        P(),
        P(),
        P(),
        P(),
        P(),
    )
    return jax.shard_map(
        by_ring if mesh.shape["enc"] == 16 else local,
        mesh=mesh,
        in_specs=placed,
        out_specs=(
            P(("groups", "enc"), None, None),
            P(("groups", "enc"), None, None),
            P(("groups", "enc"), None, None),
        ),
        check_vma=False,
    )
```

```python
import functools

import jax
import jax.numpy as jnp
from jax import lax
from jax.experimental import pallas as pl
from jax.experimental.pallas import tpu as pltpu
from jax.sharding import PartitionSpec as P


def layer_norm(values, gain_row, bias_row):
    average = jnp.mean(values, axis=-1, keepdims=True)
    centered = values - average
    variance = jnp.mean(centered * centered, axis=-1, keepdims=True)
    return centered / jnp.sqrt(variance + 1e-05) * gain_row + bias_row


def encode_patches(pixel_rows, patch_weight, position, norm_gain, norm_bias):
    leading = pixel_rows.shape[:-1]
    flat_rows = pixel_rows.reshape(-1, pixel_rows.shape[-1])
    embedded = jnp.dot(flat_rows, patch_weight, preferred_element_type=jnp.float32)
    embedded = embedded.reshape(leading + (patch_weight.shape[1],)) + position
    return layer_norm(embedded, norm_gain, norm_bias).astype(jnp.bfloat16)


def project_pairs(embed_rows, pair_weight):
    leading = embed_rows.shape[:-1]
    flat_rows = embed_rows.reshape(-1, embed_rows.shape[-1])
    projected = jnp.dot(flat_rows, pair_weight, preferred_element_type=jnp.float32)
    return projected.astype(jnp.bfloat16).reshape(leading + (pair_weight.shape[1],))


def fill_places(targets, capacity):
    count = targets.shape[0]
    item = lax.broadcasted_iota(jnp.int32, (count, count), 1)
    row = lax.broadcasted_iota(jnp.int32, (count, count), 0)
    matches = targets[:, None] == targets[None, :]
    rank = jnp.sum(jnp.where(matches & (item < row), 1, 0), axis=1).astype(jnp.int32)
    return targets * capacity + rank


def slots_of(places, width):
    count = places.shape[0]
    return places[None, :] == lax.broadcasted_iota(jnp.int32, (width, count), 0)


def hits_by_request(cache_rows, hit_owner, hit_slot, pair_weight):
    peers = lax.axis_size("enc")
    cap = max(2, 2 * hit_slot.shape[0] // peers)
    places = fill_places(hit_owner, cap)
    table = slots_of(places, peers * cap)
    wanted = jnp.sum(jnp.where(table, hit_slot[None, :], 0), axis=1).reshape(peers, cap)
    asked = lax.all_to_all(wanted, "enc", split_axis=0, concat_axis=0, tiled=True)
    stored = jnp.take(cache_rows, asked.reshape(-1), axis=0)
    stored = stored.reshape((peers, cap) + cache_rows.shape[1:])
    answered = lax.all_to_all(stored, "enc", split_axis=0, concat_axis=0, tiled=True)
    answered = answered.reshape((peers * cap,) + answered.shape[2:])
    return project_pairs(jnp.take(answered, places, axis=0), pair_weight)


MESH = pl.DeviceIdType.MESH
HALVES = 2


def ring_place(chip, chips):
    z, y = chip // 2, chip % 2
    return y * (chips - 1) + z * (1 - 2 * y)


def ring_chip(place, chips):
    y = place // (chips // 2)
    z = y * (chips - 1) + place * (1 - 2 * y)
    return 2 * z + y


def ring_kernel(
    peers,
    pixels,
    cap,
    cache_ref,
    owner_ref,
    slot_ref,
    encoder_ref,
    pixel_ref,
    patch_ref,
    position_ref,
    gain_ref,
    bias_ref,
    pair_hbm,
    hit_ref,
    miss_ref,
    fresh_ref,
    held,
    pair_ref,
    chosen,
    encoded,
    outgoing,
    incoming,
    up_send,
    up_recv,
    down_send,
    down_recv,
    side_send,
    side_recv,
    pixel_send,
    pixel_recv,
    load_sem,
    own_sem,
):
    chips = peers // 2
    slots, width = cache_ref.shape
    half = slots // HALVES
    embed = width // 2
    span = pixel_ref.shape[1] // 2
    pairs = pair_ref.shape[1]
    steps = chips - 1
    me = lax.axis_index("enc")
    chip, core = me // 2, me % 2
    place = ring_place(chip, chips)
    above = 2 * ring_chip((place + 1) % chips, chips) + core
    below = 2 * ring_chip((place + chips - 1) % chips, chips) + core
    beside = 2 * chip + 1 - core

    barrier = pltpu.get_barrier_semaphore()

    def greet(t, carry):
        pl.semaphore_signal(
            barrier, inc=1, device_id={"enc": (me + t) % peers}, device_id_type=MESH
        )
        return carry

    lax.fori_loop(1, peers, greet, 0)
    load = pltpu.make_async_copy(pair_hbm, pair_ref, load_sem)
    load.start()
    held[place, pl.ds(core * slots, slots), :] = cache_ref[...]
    count = encoder_ref.shape[1]
    named = lax.broadcasted_iota(jnp.int32, (peers, count), 0) == encoder_ref[...]
    named = jnp.where(named, 1.0, 0.0)
    item = lax.broadcasted_iota(jnp.int32, (count, count), 0)
    earlier = item < lax.broadcasted_iota(jnp.int32, (count, count), 1)
    earlier = jnp.where(earlier, 1.0, 0.0).astype(jnp.bfloat16)
    before = jnp.dot(named.astype(jnp.bfloat16), earlier, preferred_element_type=jnp.float32)
    rank = jnp.sum(named * before, axis=0, keepdims=True)
    places = encoder_ref[...].astype(jnp.float32) * cap + rank
    rows = lax.broadcasted_iota(jnp.int32, (peers * cap, count), 0).astype(jnp.float32)
    table = jnp.where(rows == places, 1.0, 0.0).astype(jnp.bfloat16)
    outgoing[...] = jnp.dot(
        table, pixel_ref[...], preferred_element_type=jnp.float32
    ).astype(jnp.bfloat16)
    pl.semaphore_wait(barrier, peers - 1)

    def chunk(owner_place, owner_core, part):
        return held.at[owner_place, pl.ds(owner_core * slots + part * half, half), :]

    def move(ref, send_sem, recv_sem, target):
        return pltpu.make_async_remote_copy(
            src_ref=ref,
            dst_ref=ref,
            send_sem=send_sem,
            recv_sem=recv_sem,
            device_id={"enc": target},
            device_id_type=MESH,
        )

    def up(j, distance):
        return move(
            chunk((place + chips - distance) % chips, core, j % 2),
            up_send.at[j],
            up_recv.at[j],
            above,
        )

    def down(j, distance):
        return move(
            chunk((place + distance) % chips, core, 1 - j % 2),
            down_send.at[j],
            down_recv.at[j],
            below,
        )

    def side(k, whose):
        if k < 2:
            ref = chunk(place, whose, k)
        elif k % 2 == 0:
            j = (k - 2) // 2
            ref = chunk((place + chips - j // 2 - 1) % chips, whose, j % 2)
        else:
            j = (k - 3) // 2
            ref = chunk((place + j // 2 + 1) % chips, whose, 1 - j % 2)
        return move(ref, side_send.at[k], side_recv.at[k], beside)

    sent = []

    def start(copy):
        copy.start()
        sent.append(copy)

    for j in range(2):
        start(up(j, 0))
        start(down(j, 0))
    for j in range(2):
        start(side(j, core))

    def pixel_copy(t, target, source):
        return pltpu.make_async_remote_copy(
            src_ref=outgoing.at[pl.ds(target * cap, cap), :],
            dst_ref=incoming.at[pl.ds(source * cap, cap), :],
            send_sem=pixel_send.at[t],
            recv_sem=pixel_recv.at[t],
            device_id={"enc": target},
            device_id_type=MESH,
        )

    def send_pixels(t, carry):
        pixel_copy(t, (me + t) % peers, me).start()
        return carry

    lax.fori_loop(1, peers, send_pixels, 0)
    own = pltpu.make_async_copy(
        outgoing.at[pl.ds(me * cap, cap), :], incoming.at[pl.ds(me * cap, cap), :], own_sem
    )
    own.start()

    def encode(values, patch):
        embedded = jnp.dot(values, patch_ref[...], preferred_element_type=jnp.float32)
        embedded = embedded + position_ref[pl.ds(patch, 1), :]
        return layer_norm(embedded, gain_ref[...][None], bias_ref[...][None]).astype(jnp.bfloat16)

    def lanes(index, size):
        return pl.ds(pl.multiple_of(index * size, size), size)

    def encode_own(patch, carry):
        encoded[:, lanes(patch, embed)] = encode(pixel_ref[:, lanes(patch, span)], patch)
        return carry

    tile = 512
    tiles = pairs // tile

    def project(source, target):
        def one(i, carry):
            patch, column = i // tiles, i % tiles
            target[:, lanes(i, tile)] = jnp.dot(
                source[:, lanes(patch, embed)],
                pair_ref[:, lanes(column, tile)],
                preferred_element_type=jnp.float32,
            ).astype(jnp.bfloat16)
            return carry

        lax.fori_loop(0, 2 * tiles, one, 0)

    block = incoming.shape[0] // 2

    def encode_fresh(i, carry):
        patch, part = i // 2, i % 2
        here = pl.ds(pl.multiple_of(part * block, block), block)
        live = incoming[here, pixels : pixels + 1].astype(jnp.float32) > 0
        fresh = encode(incoming[here, lanes(patch, span)], patch)
        fresh_ref[here, lanes(patch, embed)] = jnp.where(live, fresh, jnp.zeros_like(fresh))
        return carry

    def choose(owner_place, first):
        wanted = owner_ref[...] * slots + slot_ref[...]
        row = lax.broadcasted_iota(jnp.int32, (2 * slots, wanted.shape[1]), 0)
        row = row + ring_chip(owner_place, chips) * (2 * slots)
        pick = jnp.where(wanted == row, 1.0, 0.0).T.astype(jnp.bfloat16)

        def one(i, carry):
            found = jnp.dot(
                pick, held[owner_place, :, lanes(i, tile)], preferred_element_type=jnp.float32
            ).astype(jnp.bfloat16)
            if first:
                chosen[:, lanes(i, tile)] = found
            else:
                chosen[:, lanes(i, tile)] += found
            return carry

        lax.fori_loop(0, width // tile, one, 0)

    def wait_side(*copies):
        for k in copies:
            side(k, 1 - core).wait_recv()

    lax.fori_loop(0, 2, encode_own, 0)
    for j in range(steps):
        up(j, j // 2 + 1).wait_recv()
        if j + 2 < steps:
            start(up(j + 2, j // 2 + 1))
        start(side(2 + 2 * j, core))
        down(j, j // 2 + 1).wait_recv()
        if j + 2 < steps:
            start(down(j + 2, j // 2 + 1))
        start(side(3 + 2 * j, core))
        if j == 0:
            load.wait()
            project(encoded, miss_ref)
        elif j == 1:
            wait_side(0, 1)
            choose(place, True)
        elif j == steps - 2:

            def take_pixels(t, carry):
                pixel_copy(t, me, (me + peers - t) % peers).wait_recv()
                return carry

            lax.fori_loop(1, peers, take_pixels, 0)
            own.wait()
            lax.fori_loop(0, 4, encode_fresh, 0)
        elif j % 2 == 0:
            distance = j // 2
            wait_side(*range(4 * distance - 2, 4 * distance + 2))
            choose((place + chips - distance) % chips, False)
            choose((place + distance) % chips, False)
    wait_side(2 * steps, 2 * steps + 1)
    choose((place + chips // 2) % chips, False)
    project(chosen, hit_ref)
    for copy in sent:
        copy.wait_send()

    def end_pixels(t, carry):
        pixel_copy(t, (me + t) % peers, me).wait_send()
        return carry

    lax.fori_loop(1, peers, end_pixels, 0)


def by_ring(
    cache_rows,
    hit_owner,
    hit_slot,
    miss_pixels,
    miss_encoder,
    patch_weight,
    position,
    norm_gain,
    norm_bias,
    pair_weight,
):
    peers = lax.axis_size("enc")
    slots, patches, embed = cache_rows.shape
    hits = hit_slot.shape[0]
    count, _, pixels = miss_pixels.shape
    pairs = pair_weight.shape[1]
    cap = 2 * count // peers
    span = -(-(pixels + 1) // 128) * 128
    spare = ((0, 0), (0, 0), (0, span - pixels))
    items = jnp.pad(miss_pixels, spare, constant_values=1).reshape(count, patches * span)
    patch_rows = jnp.pad(patch_weight, ((0, span - pixels), (0, 0)))
    bf16 = jnp.bfloat16
    vmem = pl.BlockSpec(memory_space=pltpu.VMEM)
    dma = pltpu.SemaphoreType.DMA
    steps = peers // 2 - 1
    hit_pairs, miss_pairs, fresh_cache = pl.pallas_call(
        functools.partial(ring_kernel, peers, pixels, cap),
        out_shape=(
            jax.ShapeDtypeStruct((hits, patches * pairs), bf16),
            jax.ShapeDtypeStruct((count, patches * pairs), bf16),
            jax.ShapeDtypeStruct((peers * cap, patches * embed), bf16),
        ),
        in_specs=[vmem] * 9 + [pl.BlockSpec(memory_space=pl.ANY)],
        out_specs=(vmem, vmem, vmem),
        scratch_shapes=[
            pltpu.VMEM((peers // 2, 2 * slots, patches * embed), bf16),
            pltpu.VMEM(pair_weight.shape, bf16),
            pltpu.VMEM((hits, patches * embed), bf16),
            pltpu.VMEM((count, patches * embed), bf16),
            pltpu.VMEM((peers * cap, patches * span), bf16),
            pltpu.VMEM((peers * cap, patches * span), bf16),
            dma((steps,)),
            dma((steps,)),
            dma((steps,)),
            dma((steps,)),
            dma((2 * steps + 2,)),
            dma((2 * steps + 2,)),
            dma((peers,)),
            dma((peers,)),
            dma,
            dma,
        ],
        compiler_params=pltpu.CompilerParams(
            collective_id=0, has_side_effects=True, vmem_limit_bytes=44 * 1024 * 1024
        ),
        cost_estimate=pl.CostEstimate(
            flops=2 * 2 * (hits + count) * embed * pairs,
            bytes_accessed=16 * 1024 * 1024,
            transcendentals=0,
        ),
    )(
        cache_rows.reshape(slots, patches * embed),
        hit_owner.reshape(1, hits),
        hit_slot.reshape(1, hits),
        miss_encoder.reshape(1, count),
        items,
        patch_rows,
        position,
        norm_gain,
        norm_bias,
        pair_weight,
    )
    return (
        hit_pairs.reshape(hits, patches, pairs),
        miss_pairs.reshape(count, patches, pairs),
        fresh_cache.reshape(peers * cap, patches, embed),
    )


def local(
    cache_rows,
    hit_owner,
    hit_slot,
    miss_pixels,
    miss_encoder,
    patch_weight,
    position,
    norm_gain,
    norm_bias,
    pair_weight,
):
    peers = lax.axis_size("enc")
    count, patches, pixels = miss_pixels.shape
    cap = max(2, 2 * count // peers)
    width = peers * cap
    table = slots_of(fill_places(miss_encoder[:, 0], cap), width).astype(jnp.bfloat16)
    items = jnp.concatenate(
        [miss_pixels.reshape(count, patches * pixels), jnp.ones((count, 1), jnp.bfloat16)], axis=1
    )
    outgoing = jnp.dot(table, items, preferred_element_type=jnp.float32).astype(jnp.bfloat16)
    outgoing = outgoing.reshape(peers, cap, items.shape[1])
    incoming = lax.all_to_all(outgoing, "enc", split_axis=0, concat_axis=0, tiled=True)
    incoming = incoming.reshape(width, items.shape[1])
    encode = lambda rows: encode_patches(rows, patch_weight, position, norm_gain, norm_bias)
    hit_pairs = hits_by_request(cache_rows, hit_owner[:, 0], hit_slot, pair_weight)
    miss_pairs = project_pairs(encode(miss_pixels), pair_weight)
    fresh = encode(incoming[:, : patches * pixels].reshape(width, patches, pixels))
    live = incoming[:, patches * pixels :].reshape(width, 1, 1) > 0
    fresh_cache = jnp.where(live, fresh, jnp.zeros_like(fresh))
    return (hit_pairs, miss_pairs, fresh_cache)


def solution(mesh):
    placed = (
        P(("groups", "enc"), None, None),
        P(("groups", "enc"), None),
        P(("groups", "enc")),
        P(("groups", "enc"), None, None),
        P(("groups", "enc"), None),
        P(),
        P(),
        P(),
        P(),
        P(),
    )
    return jax.shard_map(
        by_ring if mesh.shape["enc"] == 16 else local,
        mesh=mesh,
        in_specs=placed,
        out_specs=(
            P(("groups", "enc"), None, None),
            P(("groups", "enc"), None, None),
            P(("groups", "enc"), None, None),
        ),
        check_vma=False,
    )
```

```python
import functools

import jax
import jax.numpy as jnp
from jax import lax
from jax.experimental import pallas as pl
from jax.experimental.pallas import tpu as pltpu
from jax.sharding import PartitionSpec as P


def layer_norm(values, gain_row, bias_row):
    average = jnp.mean(values, axis=-1, keepdims=True)
    centered = values - average
    variance = jnp.mean(centered * centered, axis=-1, keepdims=True)
    return centered / jnp.sqrt(variance + 1e-05) * gain_row + bias_row


def encode_patches(pixel_rows, patch_weight, position, norm_gain, norm_bias):
    leading = pixel_rows.shape[:-1]
    flat_rows = pixel_rows.reshape(-1, pixel_rows.shape[-1])
    embedded = jnp.dot(flat_rows, patch_weight, preferred_element_type=jnp.float32)
    embedded = embedded.reshape(leading + (patch_weight.shape[1],)) + position
    return layer_norm(embedded, norm_gain, norm_bias).astype(jnp.bfloat16)


def project_pairs(embed_rows, pair_weight):
    leading = embed_rows.shape[:-1]
    flat_rows = embed_rows.reshape(-1, embed_rows.shape[-1])
    projected = jnp.dot(flat_rows, pair_weight, preferred_element_type=jnp.float32)
    return projected.astype(jnp.bfloat16).reshape(leading + (pair_weight.shape[1],))


def fill_places(targets, capacity):
    count = targets.shape[0]
    item = lax.broadcasted_iota(jnp.int32, (count, count), 1)
    row = lax.broadcasted_iota(jnp.int32, (count, count), 0)
    matches = targets[:, None] == targets[None, :]
    rank = jnp.sum(jnp.where(matches & (item < row), 1, 0), axis=1).astype(jnp.int32)
    return targets * capacity + rank


def slots_of(places, width):
    count = places.shape[0]
    return places[None, :] == lax.broadcasted_iota(jnp.int32, (width, count), 0)


def hits_by_request(cache_rows, hit_owner, hit_slot, pair_weight):
    peers = lax.axis_size("enc")
    cap = max(2, 2 * hit_slot.shape[0] // peers)
    places = fill_places(hit_owner, cap)
    table = slots_of(places, peers * cap)
    wanted = jnp.sum(jnp.where(table, hit_slot[None, :], 0), axis=1).reshape(peers, cap)
    asked = lax.all_to_all(wanted, "enc", split_axis=0, concat_axis=0, tiled=True)
    stored = jnp.take(cache_rows, asked.reshape(-1), axis=0)
    stored = stored.reshape((peers, cap) + cache_rows.shape[1:])
    answered = lax.all_to_all(stored, "enc", split_axis=0, concat_axis=0, tiled=True)
    answered = answered.reshape((peers * cap,) + answered.shape[2:])
    return project_pairs(jnp.take(answered, places, axis=0), pair_weight)


MESH = pl.DeviceIdType.MESH
HALVES = 2


def ring_place(chip, chips):
    z, y = chip // 2, chip % 2
    return y * (chips - 1) + z * (1 - 2 * y)


def ring_chip(place, chips):
    y = place // (chips // 2)
    z = y * (chips - 1) + place * (1 - 2 * y)
    return 2 * z + y


def ring_kernel(
    peers,
    pixels,
    cap,
    cache_ref,
    owner_ref,
    slot_ref,
    encoder_ref,
    pixel_ref,
    patch_ref,
    position_ref,
    gain_ref,
    bias_ref,
    pair_hbm,
    hit_ref,
    miss_ref,
    fresh_ref,
    held,
    pair_ref,
    chosen,
    encoded,
    outgoing,
    incoming,
    up_send,
    up_recv,
    down_send,
    down_recv,
    side_send,
    side_recv,
    pixel_send,
    pixel_recv,
    load_sem,
    own_sem,
):
    chips = peers // 2
    slots, width = cache_ref.shape
    half = slots // HALVES
    embed = width // 2
    span = pixel_ref.shape[1] // 2
    pairs = pair_ref.shape[1]
    steps = chips - 1
    me = lax.axis_index("enc")
    chip, core = me // 2, me % 2
    place = ring_place(chip, chips)
    above = 2 * ring_chip((place + 1) % chips, chips) + core
    below = 2 * ring_chip((place + chips - 1) % chips, chips) + core
    beside = 2 * chip + 1 - core
    quarter = place % (chips // 2)
    cut_up = (quarter % 2) * (1 - quarter // 2)
    cut_down = (1 - quarter % 2) * (quarter // 2)
    across = 2 * ring_chip(chips - 1 - place, chips) + core
    far_up = above + cut_up * (across - above)
    far_down = below + cut_down * (across - below)
    far = 4

    barrier = pltpu.get_barrier_semaphore()

    def greet(t, carry):
        pl.semaphore_signal(
            barrier, inc=1, device_id={"enc": (me + t) % peers}, device_id_type=MESH
        )
        return carry

    lax.fori_loop(1, peers, greet, 0)
    load = pltpu.make_async_copy(pair_hbm, pair_ref, load_sem)
    load.start()
    held[place, pl.ds(core * slots, slots), :] = cache_ref[...]
    count = encoder_ref.shape[1]
    named = lax.broadcasted_iota(jnp.int32, (peers, count), 0) == encoder_ref[...]
    named = jnp.where(named, 1.0, 0.0)
    item = lax.broadcasted_iota(jnp.int32, (count, count), 0)
    earlier = item < lax.broadcasted_iota(jnp.int32, (count, count), 1)
    earlier = jnp.where(earlier, 1.0, 0.0).astype(jnp.bfloat16)
    before = jnp.dot(named.astype(jnp.bfloat16), earlier, preferred_element_type=jnp.float32)
    rank = jnp.sum(named * before, axis=0, keepdims=True)
    places = encoder_ref[...].astype(jnp.float32) * cap + rank
    rows = lax.broadcasted_iota(jnp.int32, (peers * cap, count), 0).astype(jnp.float32)
    table = jnp.where(rows == places, 1.0, 0.0).astype(jnp.bfloat16)
    outgoing[...] = jnp.dot(
        table, pixel_ref[...], preferred_element_type=jnp.float32
    ).astype(jnp.bfloat16)
    pl.semaphore_wait(barrier, peers - 1)

    def chunk(owner_place, owner_core, part):
        return held.at[owner_place, pl.ds(owner_core * slots + part * half, half), :]

    def move(ref, send_sem, recv_sem, target):
        return pltpu.make_async_remote_copy(
            src_ref=ref,
            dst_ref=ref,
            send_sem=send_sem,
            recv_sem=recv_sem,
            device_id={"enc": target},
            device_id_type=MESH,
        )

    def down_part(j):
        return 1 if j == steps - 1 else j % 2

    def up(j, distance):
        owner = place + chips - distance + (cut_up * (chips // 2) if j >= far else 0)
        return move(
            chunk(owner % chips, core, j % 2),
            up_send.at[j],
            up_recv.at[j],
            far_up if j >= far else above,
        )

    def down(j, distance):
        owner = place + distance + (cut_down * (chips // 2) if j >= far else 0)
        return move(
            chunk(owner % chips, core, down_part(j)),
            down_send.at[j],
            down_recv.at[j],
            far_down if j >= far else below,
        )

    def up_arrives(j):
        ref = chunk((place + chips - j // 2 - 1) % chips, core, j % 2)
        move(ref, up_send.at[j], up_recv.at[j], above).wait_recv()

    def down_arrives(j):
        ref = chunk((place + j // 2 + 1) % chips, core, down_part(j))
        move(ref, down_send.at[j], down_recv.at[j], below).wait_recv()

    def side(k, whose):
        if k < 2:
            ref = chunk(place, whose, k)
        elif k % 2 == 0:
            j = (k - 2) // 2
            ref = chunk((place + chips - j // 2 - 1) % chips, whose, j % 2)
        else:
            j = (k - 3) // 2
            ref = chunk((place + j // 2 + 1) % chips, whose, down_part(j))
        return move(ref, side_send.at[k], side_recv.at[k], beside)

    sent = []

    def start(copy):
        copy.start()
        sent.append(copy)

    for j in range(2):
        start(up(j, 0))
        start(down(j, 0))
    for j in range(2):
        start(side(j, core))

    def pixel_copy(t, target, source):
        return pltpu.make_async_remote_copy(
            src_ref=outgoing.at[pl.ds(target * cap, cap), :],
            dst_ref=incoming.at[pl.ds(source * cap, cap), :],
            send_sem=pixel_send.at[t],
            recv_sem=pixel_recv.at[t],
            device_id={"enc": target},
            device_id_type=MESH,
        )

    def send_pixels(t, carry):
        pixel_copy(t, (me + t) % peers, me).start()
        return carry

    lax.fori_loop(1, peers, send_pixels, 0)
    own = pltpu.make_async_copy(
        outgoing.at[pl.ds(me * cap, cap), :], incoming.at[pl.ds(me * cap, cap), :], own_sem
    )
    own.start()

    def encode(values, patch):
        embedded = jnp.dot(values, patch_ref[...], preferred_element_type=jnp.float32)
        embedded = embedded + position_ref[pl.ds(patch, 1), :]
        return layer_norm(embedded, gain_ref[...][None], bias_ref[...][None]).astype(jnp.bfloat16)

    def lanes(index, size):
        return pl.ds(pl.multiple_of(index * size, size), size)

    def encode_own(patch, carry):
        encoded[:, lanes(patch, embed)] = encode(pixel_ref[:, lanes(patch, span)], patch)
        return carry

    tile = 512
    tiles = pairs // tile

    def project(source, target):
        def one(i, carry):
            patch, column = i // tiles, i % tiles
            target[:, lanes(i, tile)] = jnp.dot(
                source[:, lanes(patch, embed)],
                pair_ref[:, lanes(column, tile)],
                preferred_element_type=jnp.float32,
            ).astype(jnp.bfloat16)
            return carry

        lax.fori_loop(0, 2 * tiles, one, 0)

    block = incoming.shape[0] // 2

    def encode_fresh(i, carry):
        patch, part = i // 2, i % 2
        here = pl.ds(pl.multiple_of(part * block, block), block)
        live = incoming[here, pixels : pixels + 1].astype(jnp.float32) > 0
        fresh = encode(incoming[here, lanes(patch, span)], patch)
        fresh_ref[here, lanes(patch, embed)] = jnp.where(live, fresh, jnp.zeros_like(fresh))
        return carry

    def choose(owner_place, first):
        wanted = owner_ref[...] * slots + slot_ref[...]
        row = lax.broadcasted_iota(jnp.int32, (2 * slots, wanted.shape[1]), 0)
        row = row + ring_chip(owner_place, chips) * (2 * slots)
        pick = jnp.where(wanted == row, 1.0, 0.0).T.astype(jnp.bfloat16)

        def one(i, carry):
            found = jnp.dot(
                pick, held[owner_place, :, lanes(i, tile)], preferred_element_type=jnp.float32
            ).astype(jnp.bfloat16)
            if first:
                chosen[:, lanes(i, tile)] = found
            else:
                chosen[:, lanes(i, tile)] += found
            return carry

        lax.fori_loop(0, width // tile, one, 0)

    def wait_side(*copies):
        for k in copies:
            side(k, 1 - core).wait_recv()

    lax.fori_loop(0, 2, encode_own, 0)
    for j in range(steps):
        up_arrives(j)
        if j + 2 < far:
            start(up(j + 2, j // 2 + 1))
        down_arrives(j)
        if far <= j + 2 < steps:
            start(up(j + 2, j // 2 + 1))
        if j + 2 < steps - 1:
            start(down(j + 2, j // 2 + 1))
        elif j + 2 == steps:
            start(down(steps - 1, steps // 2))
        start(side(2 + 2 * j, core))
        start(side(3 + 2 * j, core))
        if j == 0:
            load.wait()
            project(encoded, miss_ref)
        elif j == 1:
            wait_side(0, 1)
            choose(place, True)
        elif j == steps - 2:

            def take_pixels(t, carry):
                pixel_copy(t, me, (me + peers - t) % peers).wait_recv()
                return carry

            lax.fori_loop(1, peers, take_pixels, 0)
            own.wait()
            lax.fori_loop(0, 4, encode_fresh, 0)
        elif j % 2 == 0:
            distance = j // 2
            wait_side(*range(4 * distance - 2, 4 * distance + 2))
            choose((place + chips - distance) % chips, False)
            choose((place + distance) % chips, False)
    wait_side(2 * steps, 2 * steps + 1)
    choose((place + chips // 2) % chips, False)
    project(chosen, hit_ref)
    for copy in sent:
        copy.wait_send()

    def end_pixels(t, carry):
        pixel_copy(t, (me + t) % peers, me).wait_send()
        return carry

    lax.fori_loop(1, peers, end_pixels, 0)


def by_ring(
    cache_rows,
    hit_owner,
    hit_slot,
    miss_pixels,
    miss_encoder,
    patch_weight,
    position,
    norm_gain,
    norm_bias,
    pair_weight,
):
    peers = lax.axis_size("enc")
    slots, patches, embed = cache_rows.shape
    hits = hit_slot.shape[0]
    count, _, pixels = miss_pixels.shape
    pairs = pair_weight.shape[1]
    cap = 2 * count // peers
    span = -(-(pixels + 1) // 128) * 128
    spare = ((0, 0), (0, 0), (0, span - pixels))
    items = jnp.pad(miss_pixels, spare, constant_values=1).reshape(count, patches * span)
    patch_rows = jnp.pad(patch_weight, ((0, span - pixels), (0, 0)))
    bf16 = jnp.bfloat16
    vmem = pl.BlockSpec(memory_space=pltpu.VMEM)
    dma = pltpu.SemaphoreType.DMA
    steps = peers // 2 - 1
    hit_pairs, miss_pairs, fresh_cache = pl.pallas_call(
        functools.partial(ring_kernel, peers, pixels, cap),
        out_shape=(
            jax.ShapeDtypeStruct((hits, patches * pairs), bf16),
            jax.ShapeDtypeStruct((count, patches * pairs), bf16),
            jax.ShapeDtypeStruct((peers * cap, patches * embed), bf16),
        ),
        in_specs=[vmem] * 9 + [pl.BlockSpec(memory_space=pl.ANY)],
        out_specs=(vmem, vmem, vmem),
        scratch_shapes=[
            pltpu.VMEM((peers // 2, 2 * slots, patches * embed), bf16),
            pltpu.VMEM(pair_weight.shape, bf16),
            pltpu.VMEM((hits, patches * embed), bf16),
            pltpu.VMEM((count, patches * embed), bf16),
            pltpu.VMEM((peers * cap, patches * span), bf16),
            pltpu.VMEM((peers * cap, patches * span), bf16),
            dma((steps,)),
            dma((steps,)),
            dma((steps,)),
            dma((steps,)),
            dma((2 * steps + 2,)),
            dma((2 * steps + 2,)),
            dma((peers,)),
            dma((peers,)),
            dma,
            dma,
        ],
        compiler_params=pltpu.CompilerParams(
            collective_id=0, has_side_effects=True, vmem_limit_bytes=44 * 1024 * 1024
        ),
        cost_estimate=pl.CostEstimate(
            flops=2 * 2 * (hits + count) * embed * pairs,
            bytes_accessed=16 * 1024 * 1024,
            transcendentals=0,
        ),
    )(
        cache_rows.reshape(slots, patches * embed),
        hit_owner.reshape(1, hits),
        hit_slot.reshape(1, hits),
        miss_encoder.reshape(1, count),
        items,
        patch_rows,
        position,
        norm_gain,
        norm_bias,
        pair_weight,
    )
    return (
        hit_pairs.reshape(hits, patches, pairs),
        miss_pairs.reshape(count, patches, pairs),
        fresh_cache.reshape(peers * cap, patches, embed),
    )


def local(
    cache_rows,
    hit_owner,
    hit_slot,
    miss_pixels,
    miss_encoder,
    patch_weight,
    position,
    norm_gain,
    norm_bias,
    pair_weight,
):
    peers = lax.axis_size("enc")
    count, patches, pixels = miss_pixels.shape
    cap = max(2, 2 * count // peers)
    width = peers * cap
    table = slots_of(fill_places(miss_encoder[:, 0], cap), width).astype(jnp.bfloat16)
    items = jnp.concatenate(
        [miss_pixels.reshape(count, patches * pixels), jnp.ones((count, 1), jnp.bfloat16)], axis=1
    )
    outgoing = jnp.dot(table, items, preferred_element_type=jnp.float32).astype(jnp.bfloat16)
    outgoing = outgoing.reshape(peers, cap, items.shape[1])
    incoming = lax.all_to_all(outgoing, "enc", split_axis=0, concat_axis=0, tiled=True)
    incoming = incoming.reshape(width, items.shape[1])
    encode = lambda rows: encode_patches(rows, patch_weight, position, norm_gain, norm_bias)
    hit_pairs = hits_by_request(cache_rows, hit_owner[:, 0], hit_slot, pair_weight)
    miss_pairs = project_pairs(encode(miss_pixels), pair_weight)
    fresh = encode(incoming[:, : patches * pixels].reshape(width, patches, pixels))
    live = incoming[:, patches * pixels :].reshape(width, 1, 1) > 0
    fresh_cache = jnp.where(live, fresh, jnp.zeros_like(fresh))
    return (hit_pairs, miss_pairs, fresh_cache)


def solution(mesh):
    placed = (
        P(("groups", "enc"), None, None),
        P(("groups", "enc"), None),
        P(("groups", "enc")),
        P(("groups", "enc"), None, None),
        P(("groups", "enc"), None),
        P(),
        P(),
        P(),
        P(),
        P(),
    )
    return jax.shard_map(
        by_ring if mesh.shape["enc"] == 16 else local,
        mesh=mesh,
        in_specs=placed,
        out_specs=(
            P(("groups", "enc"), None, None),
            P(("groups", "enc"), None, None),
            P(("groups", "enc"), None, None),
        ),
        check_vma=False,
    )
```

```python
import functools

import jax
import jax.numpy as jnp
from jax import lax
from jax.experimental import pallas as pl
from jax.experimental.pallas import tpu as pltpu
from jax.sharding import PartitionSpec as P


def layer_norm(values, gain_row, bias_row):
    average = jnp.mean(values, axis=-1, keepdims=True)
    centered = values - average
    variance = jnp.mean(centered * centered, axis=-1, keepdims=True)
    return centered / jnp.sqrt(variance + 1e-05) * gain_row + bias_row


def encode_patches(pixel_rows, patch_weight, position, norm_gain, norm_bias):
    leading = pixel_rows.shape[:-1]
    flat_rows = pixel_rows.reshape(-1, pixel_rows.shape[-1])
    embedded = jnp.dot(flat_rows, patch_weight, preferred_element_type=jnp.float32)
    embedded = embedded.reshape(leading + (patch_weight.shape[1],)) + position
    return layer_norm(embedded, norm_gain, norm_bias).astype(jnp.bfloat16)


def project_pairs(embed_rows, pair_weight):
    leading = embed_rows.shape[:-1]
    flat_rows = embed_rows.reshape(-1, embed_rows.shape[-1])
    projected = jnp.dot(flat_rows, pair_weight, preferred_element_type=jnp.float32)
    return projected.astype(jnp.bfloat16).reshape(leading + (pair_weight.shape[1],))


def fill_places(targets, capacity):
    count = targets.shape[0]
    item = lax.broadcasted_iota(jnp.int32, (count, count), 1)
    row = lax.broadcasted_iota(jnp.int32, (count, count), 0)
    matches = targets[:, None] == targets[None, :]
    rank = jnp.sum(jnp.where(matches & (item < row), 1, 0), axis=1).astype(jnp.int32)
    return targets * capacity + rank


def slots_of(places, width):
    count = places.shape[0]
    return places[None, :] == lax.broadcasted_iota(jnp.int32, (width, count), 0)


def hits_by_request(cache_rows, hit_owner, hit_slot, pair_weight):
    peers = lax.axis_size("enc")
    cap = max(2, 2 * hit_slot.shape[0] // peers)
    places = fill_places(hit_owner, cap)
    table = slots_of(places, peers * cap)
    wanted = jnp.sum(jnp.where(table, hit_slot[None, :], 0), axis=1).reshape(peers, cap)
    asked = lax.all_to_all(wanted, "enc", split_axis=0, concat_axis=0, tiled=True)
    stored = jnp.take(cache_rows, asked.reshape(-1), axis=0)
    stored = stored.reshape((peers, cap) + cache_rows.shape[1:])
    answered = lax.all_to_all(stored, "enc", split_axis=0, concat_axis=0, tiled=True)
    answered = answered.reshape((peers * cap,) + answered.shape[2:])
    return project_pairs(jnp.take(answered, places, axis=0), pair_weight)


MESH = pl.DeviceIdType.MESH
HALVES = 2


def ring_place(chip, chips):
    z, y = chip // 2, chip % 2
    return y * (chips - 1) + z * (1 - 2 * y)


def ring_chip(place, chips):
    y = place // (chips // 2)
    z = y * (chips - 1) + place * (1 - 2 * y)
    return 2 * z + y


def ring_kernel(
    peers,
    pixels,
    cap,
    cache_ref,
    owner_ref,
    slot_ref,
    encoder_ref,
    pixel_ref,
    patch_ref,
    position_ref,
    gain_ref,
    bias_ref,
    pair_hbm,
    hit_ref,
    miss_ref,
    fresh_ref,
    held,
    pair_ref,
    chosen,
    encoded,
    outgoing,
    incoming,
    up_send,
    up_recv,
    down_send,
    down_recv,
    side_send,
    side_recv,
    pixel_send,
    pixel_recv,
    load_sem,
    own_sem,
):
    chips = peers // 2
    slots, width = cache_ref.shape
    half = slots // HALVES
    embed = width // 2
    span = pixel_ref.shape[1] // 2
    pairs = pair_ref.shape[1]
    steps = chips - 1
    me = lax.axis_index("enc")
    chip, core = me // 2, me % 2
    place = ring_place(chip, chips)
    above = 2 * ring_chip((place + 1) % chips, chips) + core
    below = 2 * ring_chip((place + chips - 1) % chips, chips) + core
    beside = 2 * chip + 1 - core
    quarter = place % (chips // 2)
    cut_up = (quarter % 2) * (1 - quarter // 2)
    cut_down = (1 - quarter % 2) * (quarter // 2)
    across = 2 * ring_chip(chips - 1 - place, chips) + core
    far_up = above + cut_up * (across - above)
    far_down = below + cut_down * (across - below)
    far = 4

    barrier = pltpu.get_barrier_semaphore()

    def greet(t, carry):
        pl.semaphore_signal(
            barrier, inc=1, device_id={"enc": (me + t) % peers}, device_id_type=MESH
        )
        return carry

    lax.fori_loop(1, peers, greet, 0)
    load = pltpu.make_async_copy(pair_hbm, pair_ref, load_sem)
    load.start()
    held[place, pl.ds(core * slots, slots), :] = cache_ref[...]
    count = encoder_ref.shape[1]
    named = lax.broadcasted_iota(jnp.int32, (peers, count), 0) == encoder_ref[...]
    named = jnp.where(named, 1.0, 0.0)
    item = lax.broadcasted_iota(jnp.int32, (count, count), 0)
    earlier = item < lax.broadcasted_iota(jnp.int32, (count, count), 1)
    earlier = jnp.where(earlier, 1.0, 0.0).astype(jnp.bfloat16)
    before = jnp.dot(named.astype(jnp.bfloat16), earlier, preferred_element_type=jnp.float32)
    rank = jnp.sum(named * before, axis=0, keepdims=True)
    places = encoder_ref[...].astype(jnp.float32) * cap + rank
    rows = lax.broadcasted_iota(jnp.int32, (peers * cap, count), 0).astype(jnp.float32)
    table = jnp.where(rows == places, 1.0, 0.0).astype(jnp.bfloat16)
    outgoing[...] = jnp.dot(
        table, pixel_ref[...], preferred_element_type=jnp.float32
    ).astype(jnp.bfloat16)
    pl.semaphore_wait(barrier, peers - 1)

    def chunk(owner_place, owner_core, part):
        return held.at[owner_place, pl.ds(owner_core * slots + part * half, half), :]

    def move(ref, send_sem, recv_sem, target):
        return pltpu.make_async_remote_copy(
            src_ref=ref,
            dst_ref=ref,
            send_sem=send_sem,
            recv_sem=recv_sem,
            device_id={"enc": target},
            device_id_type=MESH,
        )

    def down_part(j):
        return 1 if j == steps - 1 else j % 2

    def up(j, distance):
        owner = place + chips - distance + (cut_up * (chips // 2) if j >= far else 0)
        return move(
            chunk(owner % chips, core, j % 2),
            up_send.at[j],
            up_recv.at[j],
            far_up if j >= far else above,
        )

    def down(j, distance):
        owner = place + distance + (cut_down * (chips // 2) if j >= far else 0)
        return move(
            chunk(owner % chips, core, down_part(j)),
            down_send.at[j],
            down_recv.at[j],
            far_down if j >= far else below,
        )

    def up_arrives(j):
        ref = chunk((place + chips - j // 2 - 1) % chips, core, j % 2)
        move(ref, up_send.at[j], up_recv.at[j], above).wait_recv()

    def down_arrives(j):
        ref = chunk((place + j // 2 + 1) % chips, core, down_part(j))
        move(ref, down_send.at[j], down_recv.at[j], below).wait_recv()

    def side(k, whose):
        if k < 2:
            ref = chunk(place, whose, k)
        elif k % 2 == 0:
            j = (k - 2) // 2
            ref = chunk((place + chips - j // 2 - 1) % chips, whose, j % 2)
        else:
            j = (k - 3) // 2
            ref = chunk((place + j // 2 + 1) % chips, whose, down_part(j))
        return move(ref, side_send.at[k], side_recv.at[k], beside)

    sent = []

    def start(copy):
        copy.start()
        sent.append(copy)

    for j in range(2):
        start(up(j, 0))
        start(down(j, 0))
    for j in range(2):
        start(side(j, core))

    def pixel_copy(t, target, source):
        return pltpu.make_async_remote_copy(
            src_ref=outgoing.at[pl.ds(target * cap, cap), :],
            dst_ref=incoming.at[pl.ds(source * cap, cap), :],
            send_sem=pixel_send.at[t],
            recv_sem=pixel_recv.at[t],
            device_id={"enc": target},
            device_id_type=MESH,
        )

    def send_pixels(t, carry):
        pixel_copy(t, (me + t) % peers, me).start()
        return carry

    own = pltpu.make_async_copy(
        outgoing.at[pl.ds(me * cap, cap), :], incoming.at[pl.ds(me * cap, cap), :], own_sem
    )
    own.start()

    def encode(values, patch):
        embedded = jnp.dot(values, patch_ref[...], preferred_element_type=jnp.float32)
        embedded = embedded + position_ref[pl.ds(patch, 1), :]
        return layer_norm(embedded, gain_ref[...][None], bias_ref[...][None]).astype(jnp.bfloat16)

    def lanes(index, size):
        return pl.ds(pl.multiple_of(index * size, size), size)

    def encode_own(patch, carry):
        encoded[:, lanes(patch, embed)] = encode(pixel_ref[:, lanes(patch, span)], patch)
        return carry

    tile = 512
    tiles = pairs // tile

    def project(source, target):
        def one(i, carry):
            patch, column = i // tiles, i % tiles
            target[:, lanes(i, tile)] = jnp.dot(
                source[:, lanes(patch, embed)],
                pair_ref[:, lanes(column, tile)],
                preferred_element_type=jnp.float32,
            ).astype(jnp.bfloat16)
            return carry

        lax.fori_loop(0, 2 * tiles, one, 0)

    block = incoming.shape[0] // 2

    def encode_fresh(i, carry):
        patch, part = i // 2, i % 2
        here = pl.ds(pl.multiple_of(part * block, block), block)
        live = incoming[here, pixels : pixels + 1].astype(jnp.float32) > 0
        fresh = encode(incoming[here, lanes(patch, span)], patch)
        fresh_ref[here, lanes(patch, embed)] = jnp.where(live, fresh, jnp.zeros_like(fresh))
        return carry

    def choose(owner_place, first):
        wanted = owner_ref[...] * slots + slot_ref[...]
        row = lax.broadcasted_iota(jnp.int32, (2 * slots, wanted.shape[1]), 0)
        row = row + ring_chip(owner_place, chips) * (2 * slots)
        pick = jnp.where(wanted == row, 1.0, 0.0).T.astype(jnp.bfloat16)

        def one(i, carry):
            found = jnp.dot(
                pick, held[owner_place, :, lanes(i, tile)], preferred_element_type=jnp.float32
            ).astype(jnp.bfloat16)
            if first:
                chosen[:, lanes(i, tile)] = found
            else:
                chosen[:, lanes(i, tile)] += found
            return carry

        lax.fori_loop(0, width // tile, one, 0)

    def wait_side(*copies):
        for k in copies:
            side(k, 1 - core).wait_recv()

    lax.fori_loop(0, 2, encode_own, 0)
    for j in range(steps):
        up_arrives(j)
        if j + 2 < far:
            start(up(j + 2, j // 2 + 1))
        down_arrives(j)
        if far <= j + 2 < steps:
            start(up(j + 2, j // 2 + 1))
        if j + 2 < steps - 1:
            start(down(j + 2, j // 2 + 1))
        elif j + 2 == steps:
            start(down(steps - 1, steps // 2))
        start(side(2 + 2 * j, core))
        start(side(3 + 2 * j, core))
        if j == 3:
            lax.fori_loop(1, peers, send_pixels, 0)
        if j == 0:
            load.wait()
            project(encoded, miss_ref)
        elif j == 1:
            wait_side(0, 1)
            choose(place, True)
        elif j == steps - 2:

            def take_pixels(t, carry):
                pixel_copy(t, me, (me + peers - t) % peers).wait_recv()
                return carry

            lax.fori_loop(1, peers, take_pixels, 0)
            own.wait()
            lax.fori_loop(0, 4, encode_fresh, 0)
        elif j % 2 == 0:
            distance = j // 2
            wait_side(*range(4 * distance - 2, 4 * distance + 2))
            choose((place + chips - distance) % chips, False)
            choose((place + distance) % chips, False)
    wait_side(2 * steps, 2 * steps + 1)
    choose((place + chips // 2) % chips, False)
    project(chosen, hit_ref)
    for copy in sent:
        copy.wait_send()

    def end_pixels(t, carry):
        pixel_copy(t, (me + t) % peers, me).wait_send()
        return carry

    lax.fori_loop(1, peers, end_pixels, 0)


def by_ring(
    cache_rows,
    hit_owner,
    hit_slot,
    miss_pixels,
    miss_encoder,
    patch_weight,
    position,
    norm_gain,
    norm_bias,
    pair_weight,
):
    peers = lax.axis_size("enc")
    slots, patches, embed = cache_rows.shape
    hits = hit_slot.shape[0]
    count, _, pixels = miss_pixels.shape
    pairs = pair_weight.shape[1]
    cap = 2 * count // peers
    span = -(-(pixels + 1) // 128) * 128
    spare = ((0, 0), (0, 0), (0, span - pixels))
    items = jnp.pad(miss_pixels, spare, constant_values=1).reshape(count, patches * span)
    patch_rows = jnp.pad(patch_weight, ((0, span - pixels), (0, 0)))
    bf16 = jnp.bfloat16
    vmem = pl.BlockSpec(memory_space=pltpu.VMEM)
    dma = pltpu.SemaphoreType.DMA
    steps = peers // 2 - 1
    hit_pairs, miss_pairs, fresh_cache = pl.pallas_call(
        functools.partial(ring_kernel, peers, pixels, cap),
        out_shape=(
            jax.ShapeDtypeStruct((hits, patches * pairs), bf16),
            jax.ShapeDtypeStruct((count, patches * pairs), bf16),
            jax.ShapeDtypeStruct((peers * cap, patches * embed), bf16),
        ),
        in_specs=[vmem] * 9 + [pl.BlockSpec(memory_space=pl.ANY)],
        out_specs=(vmem, vmem, vmem),
        scratch_shapes=[
            pltpu.VMEM((peers // 2, 2 * slots, patches * embed), bf16),
            pltpu.VMEM(pair_weight.shape, bf16),
            pltpu.VMEM((hits, patches * embed), bf16),
            pltpu.VMEM((count, patches * embed), bf16),
            pltpu.VMEM((peers * cap, patches * span), bf16),
            pltpu.VMEM((peers * cap, patches * span), bf16),
            dma((steps,)),
            dma((steps,)),
            dma((steps,)),
            dma((steps,)),
            dma((2 * steps + 2,)),
            dma((2 * steps + 2,)),
            dma((peers,)),
            dma((peers,)),
            dma,
            dma,
        ],
        compiler_params=pltpu.CompilerParams(
            collective_id=0, has_side_effects=True, vmem_limit_bytes=44 * 1024 * 1024
        ),
        cost_estimate=pl.CostEstimate(
            flops=2 * 2 * (hits + count) * embed * pairs,
            bytes_accessed=16 * 1024 * 1024,
            transcendentals=0,
        ),
    )(
        cache_rows.reshape(slots, patches * embed),
        hit_owner.reshape(1, hits),
        hit_slot.reshape(1, hits),
        miss_encoder.reshape(1, count),
        items,
        patch_rows,
        position,
        norm_gain,
        norm_bias,
        pair_weight,
    )
    return (
        hit_pairs.reshape(hits, patches, pairs),
        miss_pairs.reshape(count, patches, pairs),
        fresh_cache.reshape(peers * cap, patches, embed),
    )


def local(
    cache_rows,
    hit_owner,
    hit_slot,
    miss_pixels,
    miss_encoder,
    patch_weight,
    position,
    norm_gain,
    norm_bias,
    pair_weight,
):
    peers = lax.axis_size("enc")
    count, patches, pixels = miss_pixels.shape
    cap = max(2, 2 * count // peers)
    width = peers * cap
    table = slots_of(fill_places(miss_encoder[:, 0], cap), width).astype(jnp.bfloat16)
    items = jnp.concatenate(
        [miss_pixels.reshape(count, patches * pixels), jnp.ones((count, 1), jnp.bfloat16)], axis=1
    )
    outgoing = jnp.dot(table, items, preferred_element_type=jnp.float32).astype(jnp.bfloat16)
    outgoing = outgoing.reshape(peers, cap, items.shape[1])
    incoming = lax.all_to_all(outgoing, "enc", split_axis=0, concat_axis=0, tiled=True)
    incoming = incoming.reshape(width, items.shape[1])
    encode = lambda rows: encode_patches(rows, patch_weight, position, norm_gain, norm_bias)
    hit_pairs = hits_by_request(cache_rows, hit_owner[:, 0], hit_slot, pair_weight)
    miss_pairs = project_pairs(encode(miss_pixels), pair_weight)
    fresh = encode(incoming[:, : patches * pixels].reshape(width, patches, pixels))
    live = incoming[:, patches * pixels :].reshape(width, 1, 1) > 0
    fresh_cache = jnp.where(live, fresh, jnp.zeros_like(fresh))
    return (hit_pairs, miss_pairs, fresh_cache)


def solution(mesh):
    placed = (
        P(("groups", "enc"), None, None),
        P(("groups", "enc"), None),
        P(("groups", "enc")),
        P(("groups", "enc"), None, None),
        P(("groups", "enc"), None),
        P(),
        P(),
        P(),
        P(),
        P(),
    )
    return jax.shard_map(
        by_ring if mesh.shape["enc"] == 16 else local,
        mesh=mesh,
        in_specs=placed,
        out_specs=(
            P(("groups", "enc"), None, None),
            P(("groups", "enc"), None, None),
            P(("groups", "enc"), None, None),
        ),
        check_vma=False,
    )
```

```python
import functools

import jax
import jax.numpy as jnp
from jax import lax
from jax.experimental import pallas as pl
from jax.experimental.pallas import tpu as pltpu
from jax.sharding import PartitionSpec as P


def layer_norm(values, gain_row, bias_row):
    average = jnp.mean(values, axis=-1, keepdims=True)
    centered = values - average
    variance = jnp.mean(centered * centered, axis=-1, keepdims=True)
    return centered / jnp.sqrt(variance + 1e-05) * gain_row + bias_row


def encode_patches(pixel_rows, patch_weight, position, norm_gain, norm_bias):
    leading = pixel_rows.shape[:-1]
    flat_rows = pixel_rows.reshape(-1, pixel_rows.shape[-1])
    embedded = jnp.dot(flat_rows, patch_weight, preferred_element_type=jnp.float32)
    embedded = embedded.reshape(leading + (patch_weight.shape[1],)) + position
    return layer_norm(embedded, norm_gain, norm_bias).astype(jnp.bfloat16)


def project_pairs(embed_rows, pair_weight):
    leading = embed_rows.shape[:-1]
    flat_rows = embed_rows.reshape(-1, embed_rows.shape[-1])
    projected = jnp.dot(flat_rows, pair_weight, preferred_element_type=jnp.float32)
    return projected.astype(jnp.bfloat16).reshape(leading + (pair_weight.shape[1],))


def fill_places(targets, capacity):
    count = targets.shape[0]
    item = lax.broadcasted_iota(jnp.int32, (count, count), 1)
    row = lax.broadcasted_iota(jnp.int32, (count, count), 0)
    matches = targets[:, None] == targets[None, :]
    rank = jnp.sum(jnp.where(matches & (item < row), 1, 0), axis=1).astype(jnp.int32)
    return targets * capacity + rank


def slots_of(places, width):
    count = places.shape[0]
    return places[None, :] == lax.broadcasted_iota(jnp.int32, (width, count), 0)


def hits_by_request(cache_rows, hit_owner, hit_slot, pair_weight):
    peers = lax.axis_size("enc")
    cap = max(2, 2 * hit_slot.shape[0] // peers)
    places = fill_places(hit_owner, cap)
    table = slots_of(places, peers * cap)
    wanted = jnp.sum(jnp.where(table, hit_slot[None, :], 0), axis=1).reshape(peers, cap)
    asked = lax.all_to_all(wanted, "enc", split_axis=0, concat_axis=0, tiled=True)
    stored = jnp.take(cache_rows, asked.reshape(-1), axis=0)
    stored = stored.reshape((peers, cap) + cache_rows.shape[1:])
    answered = lax.all_to_all(stored, "enc", split_axis=0, concat_axis=0, tiled=True)
    answered = answered.reshape((peers * cap,) + answered.shape[2:])
    return project_pairs(jnp.take(answered, places, axis=0), pair_weight)


MESH = pl.DeviceIdType.MESH
HALVES = 2


def ring_place(chip, chips):
    z, y = chip // 2, chip % 2
    return y * (chips - 1) + z * (1 - 2 * y)


def ring_chip(place, chips):
    y = place // (chips // 2)
    z = y * (chips - 1) + place * (1 - 2 * y)
    return 2 * z + y


def ring_kernel(
    peers,
    pixels,
    cap,
    cache_ref,
    owner_ref,
    slot_ref,
    encoder_ref,
    pixel_ref,
    patch_ref,
    position_ref,
    gain_ref,
    bias_ref,
    pair_hbm,
    hit_ref,
    miss_ref,
    fresh_ref,
    held,
    pair_ref,
    chosen,
    encoded,
    outgoing,
    incoming,
    up_send,
    up_recv,
    down_send,
    down_recv,
    side_send,
    side_recv,
    pixel_send,
    pixel_recv,
    load_sem,
    own_sem,
):
    chips = peers // 2
    slots, width = cache_ref.shape
    half = slots // HALVES
    embed = width // 2
    span = pixel_ref.shape[1] // 2
    pairs = pair_ref.shape[1]
    steps = chips - 1
    me = lax.axis_index("enc")
    chip, core = me // 2, me % 2
    place = ring_place(chip, chips)
    above = 2 * ring_chip((place + 1) % chips, chips) + core
    below = 2 * ring_chip((place + chips - 1) % chips, chips) + core
    beside = 2 * chip + 1 - core
    quarter = place % (chips // 2)
    cut_up = (quarter % 2) * (1 - quarter // 2)
    cut_down = (1 - quarter % 2) * (quarter // 2)
    across = 2 * ring_chip(chips - 1 - place, chips) + core
    far_up = above + cut_up * (across - above)
    far_down = below + cut_down * (across - below)
    far = 4

    barrier = pltpu.get_barrier_semaphore()

    def greet(t, carry):
        pl.semaphore_signal(
            barrier, inc=1, device_id={"enc": (me + t) % peers}, device_id_type=MESH
        )
        return carry

    lax.fori_loop(1, peers, greet, 0)
    load = pltpu.make_async_copy(pair_hbm, pair_ref, load_sem)
    load.start()
    held[place, pl.ds(core * slots, slots), :] = cache_ref[...]
    count = encoder_ref.shape[1]
    named = lax.broadcasted_iota(jnp.int32, (peers, count), 0) == encoder_ref[...]
    named = jnp.where(named, 1.0, 0.0)
    item = lax.broadcasted_iota(jnp.int32, (count, count), 0)
    earlier = item < lax.broadcasted_iota(jnp.int32, (count, count), 1)
    earlier = jnp.where(earlier, 1.0, 0.0).astype(jnp.bfloat16)
    before = jnp.dot(named.astype(jnp.bfloat16), earlier, preferred_element_type=jnp.float32)
    rank = jnp.sum(named * before, axis=0, keepdims=True)
    places = encoder_ref[...].astype(jnp.float32) * cap + rank
    rows = lax.broadcasted_iota(jnp.int32, (peers * cap, count), 0).astype(jnp.float32)
    table = jnp.where(rows == places, 1.0, 0.0).astype(jnp.bfloat16)
    outgoing[...] = jnp.dot(
        table, pixel_ref[...], preferred_element_type=jnp.float32
    ).astype(jnp.bfloat16)
    pl.semaphore_wait(barrier, peers - 1)

    def chunk(owner_place, owner_core, part):
        return held.at[owner_place, pl.ds(owner_core * slots + part * half, half), :]

    def move(ref, send_sem, recv_sem, target):
        return pltpu.make_async_remote_copy(
            src_ref=ref,
            dst_ref=ref,
            send_sem=send_sem,
            recv_sem=recv_sem,
            device_id={"enc": target},
            device_id_type=MESH,
        )

    def down_part(j):
        return 1 if j == steps - 1 else j % 2

    def up(j, distance):
        owner = place + chips - distance + (cut_up * (chips // 2) if j >= far else 0)
        return move(
            chunk(owner % chips, core, j % 2),
            up_send.at[j],
            up_recv.at[j],
            far_up if j >= far else above,
        )

    def down(j, distance):
        owner = place + distance + (cut_down * (chips // 2) if j >= far else 0)
        return move(
            chunk(owner % chips, core, down_part(j)),
            down_send.at[j],
            down_recv.at[j],
            far_down if j >= far else below,
        )

    def up_arrives(j):
        ref = chunk((place + chips - j // 2 - 1) % chips, core, j % 2)
        move(ref, up_send.at[j], up_recv.at[j], above).wait_recv()

    def down_arrives(j):
        ref = chunk((place + j // 2 + 1) % chips, core, down_part(j))
        move(ref, down_send.at[j], down_recv.at[j], below).wait_recv()

    def side(k, whose):
        if k < 2:
            ref = chunk(place, whose, k)
        elif k % 2 == 0:
            j = (k - 2) // 2
            ref = chunk((place + chips - j // 2 - 1) % chips, whose, j % 2)
        else:
            j = (k - 3) // 2
            ref = chunk((place + j // 2 + 1) % chips, whose, down_part(j))
        return move(ref, side_send.at[k], side_recv.at[k], beside)

    sent = []

    def start(copy):
        copy.start()
        sent.append(copy)

    for j in range(2):
        start(up(j, 0))
        start(down(j, 0))
    for j in range(2):
        start(side(j, core))

    def pixel_copy(t, target, source):
        return pltpu.make_async_remote_copy(
            src_ref=outgoing.at[pl.ds(target * cap, cap), :],
            dst_ref=incoming.at[pl.ds(source * cap, cap), :],
            send_sem=pixel_send.at[t],
            recv_sem=pixel_recv.at[t],
            device_id={"enc": target},
            device_id_type=MESH,
        )

    def send_pixels(t, carry):
        pixel_copy(t, (me + t) % peers, me).start()
        return carry

    own = pltpu.make_async_copy(
        outgoing.at[pl.ds(me * cap, cap), :], incoming.at[pl.ds(me * cap, cap), :], own_sem
    )
    own.start()

    def encode(values, patch):
        embedded = jnp.dot(values, patch_ref[...], preferred_element_type=jnp.float32)
        embedded = embedded + position_ref[pl.ds(patch, 1), :]
        return layer_norm(embedded, gain_ref[...][None], bias_ref[...][None]).astype(jnp.bfloat16)

    def lanes(index, size):
        return pl.ds(pl.multiple_of(index * size, size), size)

    def encode_own(patch, carry):
        encoded[:, lanes(patch, embed)] = encode(pixel_ref[:, lanes(patch, span)], patch)
        return carry

    tile = 512
    tiles = pairs // tile

    def project(source, target):
        def one(i, carry):
            patch, column = i // tiles, i % tiles
            target[:, lanes(i, tile)] = jnp.dot(
                source[:, lanes(patch, embed)],
                pair_ref[:, lanes(column, tile)],
                preferred_element_type=jnp.float32,
            ).astype(jnp.bfloat16)
            return carry

        lax.fori_loop(0, 2 * tiles, one, 0)

    block = incoming.shape[0] // 2

    def encode_fresh(i, carry):
        patch, part = i // 2, i % 2
        here = pl.ds(pl.multiple_of(part * block, block), block)
        live = incoming[here, pixels : pixels + 1].astype(jnp.float32) > 0
        fresh = encode(incoming[here, lanes(patch, span)], patch)
        fresh_ref[here, lanes(patch, embed)] = jnp.where(live, fresh, jnp.zeros_like(fresh))
        return carry

    def choose(owner_place, first):
        wanted = owner_ref[...] * slots + slot_ref[...]
        row = lax.broadcasted_iota(jnp.int32, (2 * slots, wanted.shape[1]), 0)
        row = row + ring_chip(owner_place, chips) * (2 * slots)
        pick = jnp.where(wanted == row, 1.0, 0.0).T.astype(jnp.bfloat16)

        def one(i, carry):
            found = jnp.dot(
                pick, held[owner_place, :, lanes(i, tile)], preferred_element_type=jnp.float32
            ).astype(jnp.bfloat16)
            if first:
                chosen[:, lanes(i, tile)] = found
            else:
                chosen[:, lanes(i, tile)] += found
            return carry

        lax.fori_loop(0, width // tile, one, 0)

    def wait_side(*copies):
        for k in copies:
            side(k, 1 - core).wait_recv()

    lax.fori_loop(0, 2, encode_own, 0)
    for j in range(steps):
        up_arrives(j)
        if j + 2 < far:
            start(up(j + 2, j // 2 + 1))
        down_arrives(j)
        if far <= j + 2 < steps:
            start(up(j + 2, j // 2 + 1))
        if j + 2 < steps - 1:
            start(down(j + 2, j // 2 + 1))
        elif j + 2 == steps:
            start(down(steps - 1, steps // 2))
        start(side(2 + 2 * j, core))
        start(side(3 + 2 * j, core))
        if j == 3:
            lax.fori_loop(1, peers, send_pixels, 0)
        if j == 0:
            load.wait()
            project(encoded, miss_ref)
        elif j == 1:
            wait_side(0, 1)
            choose(place, True)
        elif j % 2 == 0:
            distance = j // 2
            wait_side(*range(4 * distance - 2, 4 * distance + 2))
            choose((place + chips - distance) % chips, False)
            choose((place + distance) % chips, False)

    def take_pixels(t, carry):
        pixel_copy(t, me, (me + peers - t) % peers).wait_recv()
        return carry

    lax.fori_loop(1, peers, take_pixels, 0)
    own.wait()
    lax.fori_loop(0, 4, encode_fresh, 0)
    wait_side(2 * steps, 2 * steps + 1)
    choose((place + chips // 2) % chips, False)
    project(chosen, hit_ref)
    for copy in sent:
        copy.wait_send()

    def end_pixels(t, carry):
        pixel_copy(t, (me + t) % peers, me).wait_send()
        return carry

    lax.fori_loop(1, peers, end_pixels, 0)


def by_ring(
    cache_rows,
    hit_owner,
    hit_slot,
    miss_pixels,
    miss_encoder,
    patch_weight,
    position,
    norm_gain,
    norm_bias,
    pair_weight,
):
    peers = lax.axis_size("enc")
    slots, patches, embed = cache_rows.shape
    hits = hit_slot.shape[0]
    count, _, pixels = miss_pixels.shape
    pairs = pair_weight.shape[1]
    cap = 2 * count // peers
    span = -(-(pixels + 1) // 128) * 128
    spare = ((0, 0), (0, 0), (0, span - pixels))
    items = jnp.pad(miss_pixels, spare, constant_values=1).reshape(count, patches * span)
    patch_rows = jnp.pad(patch_weight, ((0, span - pixels), (0, 0)))
    bf16 = jnp.bfloat16
    vmem = pl.BlockSpec(memory_space=pltpu.VMEM)
    dma = pltpu.SemaphoreType.DMA
    steps = peers // 2 - 1
    hit_pairs, miss_pairs, fresh_cache = pl.pallas_call(
        functools.partial(ring_kernel, peers, pixels, cap),
        out_shape=(
            jax.ShapeDtypeStruct((hits, patches * pairs), bf16),
            jax.ShapeDtypeStruct((count, patches * pairs), bf16),
            jax.ShapeDtypeStruct((peers * cap, patches * embed), bf16),
        ),
        in_specs=[vmem] * 9 + [pl.BlockSpec(memory_space=pl.ANY)],
        out_specs=(vmem, vmem, vmem),
        scratch_shapes=[
            pltpu.VMEM((peers // 2, 2 * slots, patches * embed), bf16),
            pltpu.VMEM(pair_weight.shape, bf16),
            pltpu.VMEM((hits, patches * embed), bf16),
            pltpu.VMEM((count, patches * embed), bf16),
            pltpu.VMEM((peers * cap, patches * span), bf16),
            pltpu.VMEM((peers * cap, patches * span), bf16),
            dma((steps,)),
            dma((steps,)),
            dma((steps,)),
            dma((steps,)),
            dma((2 * steps + 2,)),
            dma((2 * steps + 2,)),
            dma((peers,)),
            dma((peers,)),
            dma,
            dma,
        ],
        compiler_params=pltpu.CompilerParams(
            collective_id=0, has_side_effects=True, vmem_limit_bytes=44 * 1024 * 1024
        ),
        cost_estimate=pl.CostEstimate(
            flops=2 * 2 * (hits + count) * embed * pairs,
            bytes_accessed=16 * 1024 * 1024,
            transcendentals=0,
        ),
    )(
        cache_rows.reshape(slots, patches * embed),
        hit_owner.reshape(1, hits),
        hit_slot.reshape(1, hits),
        miss_encoder.reshape(1, count),
        items,
        patch_rows,
        position,
        norm_gain,
        norm_bias,
        pair_weight,
    )
    return (
        hit_pairs.reshape(hits, patches, pairs),
        miss_pairs.reshape(count, patches, pairs),
        fresh_cache.reshape(peers * cap, patches, embed),
    )


def local(
    cache_rows,
    hit_owner,
    hit_slot,
    miss_pixels,
    miss_encoder,
    patch_weight,
    position,
    norm_gain,
    norm_bias,
    pair_weight,
):
    peers = lax.axis_size("enc")
    count, patches, pixels = miss_pixels.shape
    cap = max(2, 2 * count // peers)
    width = peers * cap
    table = slots_of(fill_places(miss_encoder[:, 0], cap), width).astype(jnp.bfloat16)
    items = jnp.concatenate(
        [miss_pixels.reshape(count, patches * pixels), jnp.ones((count, 1), jnp.bfloat16)], axis=1
    )
    outgoing = jnp.dot(table, items, preferred_element_type=jnp.float32).astype(jnp.bfloat16)
    outgoing = outgoing.reshape(peers, cap, items.shape[1])
    incoming = lax.all_to_all(outgoing, "enc", split_axis=0, concat_axis=0, tiled=True)
    incoming = incoming.reshape(width, items.shape[1])
    encode = lambda rows: encode_patches(rows, patch_weight, position, norm_gain, norm_bias)
    hit_pairs = hits_by_request(cache_rows, hit_owner[:, 0], hit_slot, pair_weight)
    miss_pairs = project_pairs(encode(miss_pixels), pair_weight)
    fresh = encode(incoming[:, : patches * pixels].reshape(width, patches, pixels))
    live = incoming[:, patches * pixels :].reshape(width, 1, 1) > 0
    fresh_cache = jnp.where(live, fresh, jnp.zeros_like(fresh))
    return (hit_pairs, miss_pairs, fresh_cache)


def solution(mesh):
    placed = (
        P(("groups", "enc"), None, None),
        P(("groups", "enc"), None),
        P(("groups", "enc")),
        P(("groups", "enc"), None, None),
        P(("groups", "enc"), None),
        P(),
        P(),
        P(),
        P(),
        P(),
    )
    return jax.shard_map(
        by_ring if mesh.shape["enc"] == 16 else local,
        mesh=mesh,
        in_specs=placed,
        out_specs=(
            P(("groups", "enc"), None, None),
            P(("groups", "enc"), None, None),
            P(("groups", "enc"), None, None),
        ),
        check_vma=False,
    )
```
